256 devices in a mesh: ia: 4 (over y), ja: 16 (over z, core), ka: 4 (over x).
Axes of the slice: x: 4, y: 4, z: 8, core: 2. Of those that a mesh axis runs over, the one named last changes fastest.
Arguments:
- tensor: bfloat16 [48, 6144, 4096], P('ka', 'ia', 'ja'), may hold values from -6 to 6
- factor_b: bfloat16 [4096, 128], P('ja', 'ia'), may hold values from -1 to 1
- factor_c: bfloat16 [48, 128], P('ka', 'ia'), may hold values from -1 to 1
Outputs:
- factor_a: float32 [6144, 128], P(('ia', 'ja', 'ka'))
The draws below stay inside these ranges and needn't reach their ends.
All inputs are finite; a program needn't handle non-finite values.
Results may differ from the reference program's by a relative error of at most 0.0003.
Values may be sent and summed in bfloat16 or wider, within the bound.
A program may use at most 64 MiB of HBM per device.

```python
import math
import jax
import jax.numpy as jnp
from jax import lax

RANK = 128
JB = 256
KB = 12
MODE_I = 6144
MODE_J = 4096
MODE_K = 48
N_JA = 16
N_KA = 4


def draw_factor_b(key, part):
    key = jax.random.fold_in(key, 11)
    first, second = jax.random.split(key, 2)
    rows = JB * N_JA
    values = jnp.clip(jax.random.normal(first, (rows, RANK), jnp.float32), -4.0, 4.0)
    common = jnp.clip(jax.random.normal(second, (rows, 1), jnp.float32), -4.0, 4.0)
    return jnp.clip((values + 0.6 * common) / math.sqrt(rows), -1.0, 1.0).astype(jnp.bfloat16)


def draw_factor_c(key, part):
    key = jax.random.fold_in(key, 23)
    first, second = jax.random.split(key, 2)
    rows = KB * N_KA
    values = jnp.clip(jax.random.normal(first, (rows, RANK), jnp.float32), -4.0, 4.0)
    common = jnp.clip(jax.random.normal(second, (rows, 1), jnp.float32), -4.0, 4.0)
    return jnp.clip((values + 0.6 * common) / math.sqrt(rows), -1.0, 1.0).astype(jnp.bfloat16)


def steps_of(key, shape, pieces, low, top_value):
    loudness = 1.0
    for dim, shards_of in pieces:
        heights = jax.random.uniform(jax.random.fold_in(jax.random.fold_in(key, 6), dim), (shards_of,), jnp.float32, low / len(pieces), top_value / len(pieces))
        loudness = loudness * jnp.repeat(jnp.exp(heights), shape[dim] // shards_of).reshape((-1,) + (1,) * (len(shape) - 1 - dim))
    return loudness


def noise(stream_key, dims, spread, most, cuts=(), kind=jnp.bfloat16):
    drawn = spread * jax.random.normal(stream_key, dims, jnp.float32)
    if cuts:
        drawn = drawn * steps_of(stream_key, dims, cuts, -0.22, 0.18)
    return jnp.clip(drawn, -most, most).astype(kind)


def setup_inputs(seed: int = 0) -> dict:
    arg_keys = jax.random.split(jax.random.key(seed), 4)
    tensor = noise(arg_keys[0], (MODE_K, MODE_I, MODE_J), 1.0, 6.0, ((0, 4), (1, 4), (2, 16)))
    factor_b = draw_factor_b(jax.random.fold_in(arg_keys[3], 71), 0)
    factor_c = draw_factor_c(jax.random.fold_in(arg_keys[3], 71), 0)
    return {"tensor": tensor, "factor_b": factor_b, "factor_c": factor_c}


LAMBDA_REG = 0.5

def reference(tensor, factor_b, factor_c):
    gram_b = jnp.dot(factor_b.T.astype(jnp.float32), factor_b.astype(jnp.float32), preferred_element_type=jnp.float32)
    gram_c = jnp.dot(factor_c.T.astype(jnp.float32), factor_c.astype(jnp.float32), preferred_element_type=jnp.float32)
    rank_cols = factor_b.shape[1]
    gram = gram_b * gram_c + LAMBDA_REG * jnp.eye(rank_cols, dtype=jnp.float32)

    def accumulate(total, pair):
        slab, crow = pair
        term = jnp.dot(slab.astype(jnp.float32), factor_b.astype(jnp.float32), preferred_element_type=jnp.float32)
        return (total + term * crow.astype(jnp.float32)[None, :], None)
    start = jnp.zeros((tensor.shape[1], rank_cols), jnp.float32)
    mttkrp, unused = lax.scan(accumulate, start, (tensor, factor_c))
    lower = jnp.linalg.cholesky(gram)
    middle = lax.linalg.triangular_solve(lower, mttkrp.T, left_side=True, lower=True)
    solved = lax.linalg.triangular_solve(lower, middle, left_side=True, lower=True, transpose_a=True)
    return solved.T
```

```python
import jax
import jax.numpy as jnp
from jax import lax
from jax.experimental import pallas as pl
from jax.experimental.pallas import tpu as pltpu
from jax.sharding import PartitionSpec as P

LAMBDA_REG = 0.5
MESH = pl.DeviceIdType.MESH
F32 = jnp.float32
BF16 = jnp.bfloat16
EXACT = lax.Precision.HIGHEST

R = 128
NIA, NJA, NKA = 4, 16, 4
NZ = NJA // 2
KB, IB, JB = 12, 1536, 256
ROWS = IB // (NJA * NKA)
BLOCK = ROWS * NKA
PLANE = NIA * NKA
GROWS = R // PLANE
TERMS = 8
SURE = 2e-4


def nt(a, b):
    return lax.dot_general(a, b, (((1,), (1,)), ((), ())), preferred_element_type=F32)


def tn(a, b):
    return lax.dot_general(a, b, (((0,), (0,)), ((), ())), preferred_element_type=F32)


def exact(a, b):
    return jnp.dot(a, b, preferred_element_type=F32, precision=EXACT)


def eye():
    i = lax.broadcasted_iota(jnp.int32, (R, R), 0)
    j = lax.broadcasted_iota(jnp.int32, (R, R), 1)
    return (i == j).astype(F32)


def fused(
    t_hbm, b_hbm, c_hbm, y_out, m_out, g_out, r_out,
    t_v, b_v, c_v, wide, gat, bfull, call, gpart, growin, gram,
    psend, precv, own, xin, zown, zin,
    t_sem, in_sem, a_send, a_recv, c_send, c_recv, g_send, g_recv, h_send, h_recv,
    p_send, p_recv, x_send, x_recv, z_send, z_recv,
):
    ia, ja, ka = lax.axis_index("ia"), lax.axis_index("ja"), lax.axis_index("ka")
    z, core = ja // 2, lax.rem(ja, 2)
    other = 1 - core
    plane = ia * NKA + ka

    load_b = pltpu.make_async_copy(b_hbm, b_v, in_sem.at[0])
    load_c = pltpu.make_async_copy(c_hbm, c_v, in_sem.at[1])
    load_b.start()
    load_c.start()
    loads = [pltpu.make_async_copy(t_hbm.at[k], t_v.at[k], t_sem.at[k]) for k in range(KB)]
    for load in loads:
        load.start()

    barrier = pltpu.get_barrier_semaphore()

    def greet_ja(o, carry):
        pl.semaphore_signal(
            barrier, inc=1, device_id=(ia, lax.rem(ja + o, NJA), ka), device_id_type=MESH
        )
        return carry

    def greet_plane(o, carry):
        p = lax.rem(plane + o, PLANE)
        pl.semaphore_signal(
            barrier, inc=1, device_id=(p // NKA, ja, lax.rem(p, NKA)), device_id_type=MESH
        )
        return carry

    lax.fori_loop(1, NJA, greet_ja, 0)
    lax.fori_loop(1, PLANE, greet_plane, 0)

    load_b.wait()
    load_c.wait()
    wide[0:JB, :] = b_v[...].astype(F32)
    wide[JB:, :] = jnp.zeros((R, R // NIA), F32)
    wide[JB : JB + KB, :] = c_v[...].astype(F32)
    gat[ia] = wide[...].T.astype(BF16)
    pl.semaphore_wait(barrier, NJA - 1 + PLANE - 1)

    for o in range(1, NIA):
        pltpu.make_async_remote_copy(
            gat.at[ia], gat.at[ia], a_send, a_recv,
            device_id=(lax.rem(ia + o, NIA), ja, ka), device_id_type=MESH,
        ).start()
    pltpu.make_async_copy(gat.at[0:3], gat.at[0:3], a_recv).wait()
    pltpu.make_async_copy(gat.at[0:3], gat.at[0:3], a_send).wait()

    both = gat[...].reshape(R, JB + R)
    bt = both[:, :JB]
    gpart[...] = nt(bt, bt)
    bfull[...] = bt.astype(F32).T.astype(BF16)
    crows = both[:, JB:].astype(F32).T[0:16]
    call[ka] = crows.astype(BF16)

    mine = pl.multiple_of(plane * GROWS, GROWS)

    def send_rows(o, carry):
        pltpu.make_async_remote_copy(
            gpart.at[pl.ds(mine, GROWS)], growin.at[o - 1], g_send, g_recv,
            device_id=(ia, lax.rem(ja + o, NJA), ka), device_id_type=MESH,
        ).start()
        return carry

    lax.fori_loop(1, NJA, send_rows, 0)
    for o in range(1, NKA):
        pltpu.make_async_remote_copy(
            call.at[ka], call.at[ka], c_send, c_recv,
            device_id=(ia, ja, lax.rem(ka + o, NKA)), device_id_type=MESH,
        ).start()

    for load in loads:
        load.wait()
    b_all = bfull[...]
    scales = [crows[k : k + 1] for k in range(KB)]

    def contract(rows):
        t = t_v[:, pl.ds(rows, BLOCK), :].reshape(KB * BLOCK, JB)
        products = jnp.dot(t, b_all, preferred_element_type=F32)
        total = products[0:BLOCK] * scales[0]
        for k in range(1, KB):
            total = total + products[k * BLOCK : (k + 1) * BLOCK] * scales[k]
        return total

    def pair_copy(i):
        return pltpu.make_async_remote_copy(
            psend.at[i], precv.at[i], p_send.at[i], p_recv.at[i],
            device_id=(ia, 2 * z + other, ka), device_id_type=MESH,
        )

    def sibling_block(i, carry):
        psend[i] = contract(pl.multiple_of((2 * i + other) * BLOCK, BLOCK))
        pair_copy(i).start()
        return carry

    lax.fori_loop(0, NZ, sibling_block, 0)

    pltpu.make_async_copy(growin, growin, g_recv).wait()
    rows = gpart[pl.ds(mine, GROWS), :]
    for o in range(NJA - 1):
        rows = rows + growin[o]
    gram[pl.ds(mine, GROWS), :] = rows

    def send_gram(o, carry):
        p = lax.rem(plane + o, PLANE)
        pltpu.make_async_remote_copy(
            gram.at[pl.ds(mine, GROWS)], gram.at[pl.ds(mine, GROWS)], h_send, h_recv,
            device_id=(p // NKA, ja, lax.rem(p, NKA)), device_id_type=MESH,
        ).start()
        return carry

    lax.fori_loop(1, PLANE, send_gram, 0)

    def own_block(i, carry):
        total = contract(pl.multiple_of((2 * i + core) * BLOCK, BLOCK))
        pair_copy(i).wait_recv()
        own[i] = total + precv[i]
        for o in range(1, NKA):
            to = lax.rem(ka + o, NKA)
            pltpu.make_async_remote_copy(
                own.at[i, pl.ds(pl.multiple_of(to * ROWS, ROWS), ROWS)], xin.at[o - 1, i],
                x_send, x_recv, device_id=(ia, ja, to), device_id_type=MESH,
            ).start()
        return carry

    lax.fori_loop(0, NZ, own_block, 0)

    pltpu.make_async_copy(gram.at[0 : R - GROWS], gram.at[0 : R - GROWS], h_recv).wait()
    pltpu.make_async_copy(call.at[0:3], call.at[0:3], c_recv).wait()
    every = call[...].reshape(NKA * 16, R)
    one = eye()
    g = gram[...] * tn(every, every) + LAMBDA_REG * one
    g_out[...] = g
    bound = jnp.max(jnp.sum(jnp.abs(g), axis=0, keepdims=True), axis=1, keepdims=True)
    alpha = 2.0 / (bound + LAMBDA_REG)
    e = one - alpha * g
    p = one + e
    for _ in range(TERMS - 1):
        e = exact(e, e)
        p = p + exact(p, e)
    inv = alpha * p
    rest = one - exact(g, inv)
    r_out[...] = jnp.broadcast_to(
        jnp.max(jnp.sum(jnp.abs(rest), axis=0, keepdims=True), axis=1, keepdims=True), (8, R)
    )
    inv = inv + exact(inv, rest)

    pltpu.make_async_copy(xin, xin, x_recv).wait()
    place = pl.ds(pl.multiple_of(ka * ROWS, ROWS), ROWS)
    for i in range(NZ):
        zown[i] = own[i, place, :] + xin[0, i] + xin[1, i] + xin[2, i]
    for o in range(1, NZ):
        to = lax.rem(z + o, NZ)
        pltpu.make_async_remote_copy(
            zown.at[to], zin.at[o - 1], z_send, z_recv,
            device_id=(ia, 2 * to + core, ka), device_id_type=MESH,
        ).start()
    pltpu.make_async_copy(zin, zin, z_recv).wait()
    m = zown[z]
    for o in range(NZ - 1):
        m = m + zin[o]
    m_out[...] = m
    y_out[...] = exact(m, inv)

    pltpu.make_async_copy(growin, growin, g_send).wait()
    pltpu.make_async_copy(call.at[0:3], call.at[0:3], c_send).wait()
    pltpu.make_async_copy(gram.at[0 : R - GROWS], gram.at[0 : R - GROWS], h_send).wait()
    for i in range(NZ):
        pair_copy(i).wait_send()
    pltpu.make_async_copy(xin, xin, x_send).wait()
    pltpu.make_async_copy(zin, zin, z_send).wait()


def finish(y_ref, r_ref, m_ref, g_ref, out_ref, mat, rhs, upper, sem):
    sure = jnp.max(r_ref[...]) < SURE

    @pl.when(sure)
    def _():
        out_ref[...] = y_ref[...]

    @pl.when(jnp.logical_not(sure))
    def _():
        rhs[...] = jnp.zeros((R, R), F32)
        load_g = pltpu.make_async_copy(g_ref, mat, sem.at[0])
        load_m = pltpu.make_async_copy(m_ref, rhs.at[0:ROWS], sem.at[1])
        load_g.start()
        load_m.start()
        load_g.wait()
        load_m.wait()
        rhs[...] = rhs[...].T
        down = lax.broadcasted_iota(jnp.int32, (R, 1), 0)
        across = lax.broadcasted_iota(jnp.int32, (1, R), 1)

        def column(a, k):
            return jnp.sum(jnp.where(across == k, a, 0.0), axis=1, keepdims=True)

        def forward(k, carry):
            a = mat[...]
            row = mat[pl.ds(k, 1), :]
            root = jnp.sqrt(jnp.sum(jnp.where(across == k, row, 0.0), axis=1, keepdims=True))
            lrow = jnp.where(across >= k, row / root, 0.0)
            lcol = jnp.where(down > k, column(a, k) / root, 0.0)
            upper[pl.ds(k, 1), :] = lrow
            mat[...] = a - lcol * lrow
            b = rhs[pl.ds(k, 1), :] / root
            rhs[...] = jnp.where(down == k, b, rhs[...] - lcol * b)
            return carry

        lax.fori_loop(0, R, forward, 0)

        def backward(step, carry):
            k = R - 1 - step
            col = column(upper[...], k)
            root = jnp.sum(jnp.where(down == k, col, 0.0), axis=0, keepdims=True)
            x = rhs[pl.ds(k, 1), :] / root
            rhs[...] = jnp.where(
                down == k, x, rhs[...] - jnp.where(down < k, col, 0.0) * x
            )
            return carry

        lax.fori_loop(0, R, backward, 0)
        out_ref[...] = rhs[...].T[0:ROWS]


def body(tensor, factor_b, factor_c):
    vmem = pl.BlockSpec(memory_space=pltpu.VMEM)
    hbm = pl.BlockSpec(memory_space=pltpu.HBM)
    dma = pltpu.SemaphoreType.DMA
    y, m, g, r = pl.pallas_call(
        fused,
        out_shape=[
            jax.ShapeDtypeStruct((ROWS, R), F32),
            jax.ShapeDtypeStruct((ROWS, R), F32),
            jax.ShapeDtypeStruct((R, R), F32),
            jax.ShapeDtypeStruct((8, R), F32),
        ],
        in_specs=[hbm, hbm, hbm],
        out_specs=[vmem] * 4,
        scratch_shapes=[
            pltpu.VMEM((KB, IB, JB), BF16),
            pltpu.VMEM((JB, R // NIA), BF16),
            pltpu.VMEM((KB, R // NIA), BF16),
            pltpu.VMEM((JB + R, R // NIA), F32),
            pltpu.VMEM((NIA, R // NIA, JB + R), BF16),
            pltpu.VMEM((JB, R), BF16),
            pltpu.VMEM((NKA, 16, R), BF16),
            pltpu.VMEM((R, R), F32),
            pltpu.VMEM((NJA - 1, GROWS, R), F32),
            pltpu.VMEM((R, R), F32),
            pltpu.VMEM((NZ, BLOCK, R), F32),
            pltpu.VMEM((NZ, BLOCK, R), F32),
            pltpu.VMEM((NZ, BLOCK, R), F32),
            pltpu.VMEM((NKA - 1, NZ, ROWS, R), F32),
            pltpu.VMEM((NZ, ROWS, R), F32),
            pltpu.VMEM((NZ - 1, ROWS, R), F32),
            dma((KB,)),
            dma((2,)),
            dma, dma, dma, dma, dma, dma, dma, dma,
            dma((NZ,)),
            dma((NZ,)),
            dma, dma, dma, dma,
        ],
        compiler_params=pltpu.CompilerParams(
            collective_id=0, has_side_effects=True, vmem_limit_bytes=40 * 1024 * 1024
        ),
    )(tensor, factor_b, factor_c)
    return pl.pallas_call(
        finish,
        out_shape=jax.ShapeDtypeStruct((ROWS, R), F32),
        in_specs=[vmem, vmem, hbm, hbm],
        out_specs=vmem,
        scratch_shapes=[
            pltpu.VMEM((R, R), F32),
            pltpu.VMEM((R, R), F32),
            pltpu.VMEM((R, R), F32),
            dma((2,)),
        ],
    )(y, r, m, g)


def solution(mesh):
    return jax.shard_map(
        body,
        mesh=mesh,
        in_specs=(P("ka", "ia", "ja"), P("ja", "ia"), P("ka", "ia")),
        out_specs=P(("ia", "ja", "ka"), None),
        check_vma=False,
    )
```

```python
import jax
import jax.numpy as jnp
from jax import lax
from jax.experimental import pallas as pl
from jax.experimental.pallas import tpu as pltpu
from jax.sharding import PartitionSpec as P

LAMBDA_REG = 0.5
MESH = pl.DeviceIdType.MESH
F32 = jnp.float32
BF16 = jnp.bfloat16
EXACT = lax.Precision.HIGHEST

R = 128
NIA, NJA, NKA = 4, 16, 4
NZ = NJA // 2
KB, IB, JB = 12, 1536, 256
ROWS = IB // (NJA * NKA)
BLOCK = ROWS * NKA
PLANE = NIA * NKA
GROWS = R // PLANE
TERMS = 7
R_AT, M_AT, G_AT = ROWS, ROWS + 8, 2 * ROWS + 8
SURE = 2e-4


def nt(a, b):
    return lax.dot_general(a, b, (((1,), (1,)), ((), ())), preferred_element_type=F32)


def tn(a, b):
    return lax.dot_general(a, b, (((0,), (0,)), ((), ())), preferred_element_type=F32)


def exact(a, b):
    return jnp.dot(a, b, preferred_element_type=F32, precision=EXACT)


def eye():
    i = lax.broadcasted_iota(jnp.int32, (R, R), 0)
    j = lax.broadcasted_iota(jnp.int32, (R, R), 1)
    return (i == j).astype(F32)


def split(a):
    high = a.astype(BF16)
    return high, (a - high.astype(F32)).astype(BF16)


def mul3(a, b):
    dot = lambda u, v: jnp.dot(u, v, preferred_element_type=F32)
    return dot(a[0], b[0]) + (dot(a[0], b[1]) + dot(a[1], b[0]))


def fused(
    t_hbm, b_hbm, c_hbm, pack,
    t_v, c_v, gat, cin, bfull, call, gpart, growin, gram,
    psend, precv, own, xin, zown, zin,
    t_sem, in_sem, a_send, a_recv, d_send, d_recv, c_send, c_recv, g_send, g_recv, h_send, h_recv,
    p_send, p_recv, x_send, x_recv, z_send, z_recv,
):
    ia, ja, ka = lax.axis_index("ia"), lax.axis_index("ja"), lax.axis_index("ka")
    z, core = ja // 2, lax.rem(ja, 2)
    other = 1 - core
    plane = ia * NKA + ka
    left = []

    def drain():
        for f in left:
            f()

    load_b = pltpu.make_async_copy(b_hbm, gat.at[ia], in_sem.at[0])
    load_c = pltpu.make_async_copy(c_hbm, c_v, in_sem.at[1])
    load_b.start()
    load_c.start()
    loads = [pltpu.make_async_copy(t_hbm.at[k], t_v.at[k], t_sem.at[k]) for k in range(KB)]
    for load in loads:
        load.start()
        left.append(load.wait)

    barrier = pltpu.get_barrier_semaphore()

    def greet_ja(o, carry):
        pl.semaphore_signal(
            barrier, inc=1, device_id=(ia, lax.rem(ja + o, NJA), ka), device_id_type=MESH
        )
        return carry

    def greet_plane(o, carry):
        p = lax.rem(plane + o, PLANE)
        pl.semaphore_signal(
            barrier, inc=1, device_id=(p // NKA, ja, lax.rem(p, NKA)), device_id_type=MESH
        )
        return carry

    lax.fori_loop(1, NJA, greet_ja, 0)
    lax.fori_loop(1, PLANE, greet_plane, 0)

    load_c.wait()
    lane = lax.broadcasted_iota(jnp.int32, (KB, R), 1)
    c4 = jnp.concatenate([c_v[...].astype(F32)] * NIA, axis=1)
    cin[ia] = jnp.zeros((16, R), F32)
    cin[ia, 0:KB, :] = jnp.where(lane // (R // NIA) == ia, c4, 0.0)
    load_b.wait()
    pl.semaphore_wait(barrier, NJA - 1 + PLANE - 1)

    for o in range(1, NIA):
        to = (lax.rem(ia + o, NIA), ja, ka)
        pltpu.make_async_remote_copy(
            gat.at[ia], gat.at[ia], a_send, a_recv, device_id=to, device_id_type=MESH
        ).start()
        pltpu.make_async_remote_copy(
            cin.at[ia], cin.at[ia], d_send, d_recv, device_id=to, device_id_type=MESH
        ).start()
    pltpu.make_async_copy(gat.at[0:3], gat.at[0:3], a_recv).wait()
    left.append(pltpu.make_async_copy(gat.at[0:3], gat.at[0:3], a_send).wait)
    left.append(pltpu.make_async_copy(cin.at[0:3], cin.at[0:3], d_send).wait)

    bt = gat[...].reshape(R, JB)
    gpart[...] = nt(bt, bt)
    bfull[...] = bt.astype(F32).T.astype(BF16)
    pltpu.make_async_copy(cin.at[0:3], cin.at[0:3], d_recv).wait()
    crows = cin[0] + cin[1] + cin[2] + cin[3]
    call[ka] = crows

    mine = pl.multiple_of(plane * GROWS, GROWS)

    def send_rows(o, carry):
        pltpu.make_async_remote_copy(
            gpart.at[pl.ds(mine, GROWS)], growin.at[o - 1], g_send, g_recv,
            device_id=(ia, lax.rem(ja + o, NJA), ka), device_id_type=MESH,
        ).start()
        return carry

    lax.fori_loop(1, NJA, send_rows, 0)
    for o in range(1, NKA):
        pltpu.make_async_remote_copy(
            call.at[ka], call.at[ka], c_send, c_recv,
            device_id=(ia, ja, lax.rem(ka + o, NKA)), device_id_type=MESH,
        ).start()
    left.append(pltpu.make_async_copy(growin, growin, g_send).wait)
    left.append(pltpu.make_async_copy(call.at[0:3], call.at[0:3], c_send).wait)

    for load in loads:
        load.wait()
        left.remove(load.wait)
    b_all = bfull[...]
    scales = [crows[k : k + 1] for k in range(KB)]

    def contract(rows):
        t = t_v[:, pl.ds(rows, BLOCK), :].reshape(KB * BLOCK, JB)
        products = jnp.dot(t, b_all, preferred_element_type=F32)
        total = products[0:BLOCK] * scales[0]
        for k in range(1, KB):
            total = total + products[k * BLOCK : (k + 1) * BLOCK] * scales[k]
        return total

    def pair_copy(i):
        return pltpu.make_async_remote_copy(
            psend.at[i], precv.at[i], p_send.at[i], p_recv.at[i],
            device_id=(ia, 2 * z + other, ka), device_id_type=MESH,
        )

    def sibling_block(i, carry):
        psend[i] = contract(pl.multiple_of((2 * i + other) * BLOCK, BLOCK))
        pair_copy(i).start()
        return carry

    lax.fori_loop(0, NZ, sibling_block, 0)
    left.append(lambda: [pair_copy(i).wait_send() for i in range(NZ)])

    def own_block(i, carry):
        total = contract(pl.multiple_of((2 * i + core) * BLOCK, BLOCK))
        pair_copy(i).wait_recv()
        own[i] = total + precv[i]
        for o in range(1, NKA):
            to = lax.rem(ka + o, NKA)
            pltpu.make_async_remote_copy(
                own.at[i, pl.ds(pl.multiple_of(to * ROWS, ROWS), ROWS)], xin.at[o - 1, i],
                x_send, x_recv, device_id=(ia, ja, to), device_id_type=MESH,
            ).start()
        return carry

    lax.fori_loop(0, NZ, own_block, 0)
    left.append(pltpu.make_async_copy(xin, xin, x_send).wait)

    pltpu.make_async_copy(growin, growin, g_recv).wait()
    rows = gpart[pl.ds(mine, GROWS), :]
    for o in range(NJA - 1):
        rows = rows + growin[o]
    gram[pl.ds(mine, GROWS), :] = rows

    def send_gram(o, carry):
        p = lax.rem(plane + o, PLANE)
        pltpu.make_async_remote_copy(
            gram.at[pl.ds(mine, GROWS)], gram.at[pl.ds(mine, GROWS)], h_send, h_recv,
            device_id=(p // NKA, ja, lax.rem(p, NKA)), device_id_type=MESH,
        ).start()
        return carry

    lax.fori_loop(1, PLANE, send_gram, 0)
    left.append(pltpu.make_async_copy(gram.at[0 : R - GROWS], gram.at[0 : R - GROWS], h_send).wait)

    pltpu.make_async_copy(xin, xin, x_recv).wait()
    place = pl.ds(pl.multiple_of(ka * ROWS, ROWS), ROWS)
    for i in range(NZ):
        zown[i] = own[i, place, :] + xin[0, i] + xin[1, i] + xin[2, i]
    for o in range(1, NZ):
        to = lax.rem(z + o, NZ)
        pltpu.make_async_remote_copy(
            zown.at[to], zin.at[o - 1], z_send, z_recv,
            device_id=(ia, 2 * to + core, ka), device_id_type=MESH,
        ).start()
    left.append(pltpu.make_async_copy(zin, zin, z_send).wait)
    pltpu.make_async_copy(gram.at[0 : R - GROWS], gram.at[0 : R - GROWS], h_recv).wait()
    pltpu.make_async_copy(call.at[0:3], call.at[0:3], c_recv).wait()
    every = call[...].reshape(NKA * 16, R).astype(BF16)
    one = eye()
    g = gram[...] * tn(every, every) + LAMBDA_REG * one
    pack[G_AT:, :] = g
    bound = jnp.max(jnp.sum(jnp.abs(g), axis=0, keepdims=True), axis=1, keepdims=True)
    alpha = 2.0 / (bound + LAMBDA_REG)
    e = one - alpha * g
    p = one + e
    for _ in range(TERMS - 1):
        parts = split(e)
        e = mul3(parts, parts)
        p = p + mul3(split(p), split(e))
    inv = alpha * p
    rest = one - exact(g, inv)
    pack[R_AT : R_AT + 8, :] = jnp.broadcast_to(
        jnp.max(jnp.sum(jnp.abs(rest), axis=0, keepdims=True), axis=1, keepdims=True), (8, R)
    )
    inv = inv + exact(inv, rest)

    pltpu.make_async_copy(zin, zin, z_recv).wait()
    m = zown[z]
    for o in range(NZ - 1):
        m = m + zin[o]
    pack[M_AT : M_AT + ROWS, :] = m
    pack[0:ROWS, :] = exact(m, inv)
    drain()


def finish(pack, out_ref, head, mat, rhs, upper, sem):
    load = pltpu.make_async_copy(pack.at[0:M_AT], head, sem.at[0])
    load.start()
    load.wait()
    sure = jnp.max(head[R_AT:M_AT, :]) < SURE

    @pl.when(sure)
    def _():
        out_ref[...] = head[0:ROWS, :]

    @pl.when(jnp.logical_not(sure))
    def _():
        rhs[...] = jnp.zeros((R, R), F32)
        load_g = pltpu.make_async_copy(pack.at[G_AT:], mat, sem.at[0])
        load_m = pltpu.make_async_copy(pack.at[M_AT:G_AT], rhs.at[0:ROWS], sem.at[1])
        load_g.start()
        load_m.start()
        load_g.wait()
        load_m.wait()
        rhs[...] = rhs[...].T
        down = lax.broadcasted_iota(jnp.int32, (R, 1), 0)
        across = lax.broadcasted_iota(jnp.int32, (1, R), 1)

        def column(a, k):
            return jnp.sum(jnp.where(across == k, a, 0.0), axis=1, keepdims=True)

        def forward(k, carry):
            a = mat[...]
            row = mat[pl.ds(k, 1), :]
            root = jnp.sqrt(jnp.sum(jnp.where(across == k, row, 0.0), axis=1, keepdims=True))
            lrow = jnp.where(across >= k, row / root, 0.0)
            lcol = jnp.where(down > k, column(a, k) / root, 0.0)
            upper[pl.ds(k, 1), :] = lrow
            mat[...] = a - lcol * lrow
            b = rhs[pl.ds(k, 1), :] / root
            rhs[...] = jnp.where(down == k, b, rhs[...] - lcol * b)
            return carry

        lax.fori_loop(0, R, forward, 0)

        def backward(step, carry):
            k = R - 1 - step
            col = column(upper[...], k)
            root = jnp.sum(jnp.where(down == k, col, 0.0), axis=0, keepdims=True)
            x = rhs[pl.ds(k, 1), :] / root
            rhs[...] = jnp.where(
                down == k, x, rhs[...] - jnp.where(down < k, col, 0.0) * x
            )
            return carry

        lax.fori_loop(0, R, backward, 0)
        out_ref[...] = rhs[...].T[0:ROWS]


def body(tensor, factor_b, factor_c):
    vmem = pl.BlockSpec(memory_space=pltpu.VMEM)
    hbm = pl.BlockSpec(memory_space=pltpu.HBM)
    dma = pltpu.SemaphoreType.DMA
    pack = pl.pallas_call(
        fused,
        out_shape=jax.ShapeDtypeStruct((G_AT + R, R), F32),
        in_specs=[hbm, hbm, hbm],
        out_specs=vmem,
        scratch_shapes=[
            pltpu.VMEM((KB, IB, JB), BF16),
            pltpu.VMEM((KB, R // NIA), BF16),
            pltpu.VMEM((NIA, R // NIA, JB), BF16),
            pltpu.VMEM((NIA, 16, R), F32),
            pltpu.VMEM((JB, R), BF16),
            pltpu.VMEM((NKA, 16, R), F32),
            pltpu.VMEM((R, R), F32),
            pltpu.VMEM((NJA - 1, GROWS, R), F32),
            pltpu.VMEM((R, R), F32),
            pltpu.VMEM((NZ, BLOCK, R), F32),
            pltpu.VMEM((NZ, BLOCK, R), F32),
            pltpu.VMEM((NZ, BLOCK, R), F32),
            pltpu.VMEM((NKA - 1, NZ, ROWS, R), F32),
            pltpu.VMEM((NZ, ROWS, R), F32),
            pltpu.VMEM((NZ - 1, ROWS, R), F32),
            dma((KB,)),
            dma((2,)),
            dma, dma, dma, dma, dma, dma, dma, dma, dma, dma,
            dma((NZ,)),
            dma((NZ,)),
            dma, dma, dma, dma,
        ],
        compiler_params=pltpu.CompilerParams(
            collective_id=0, has_side_effects=True, vmem_limit_bytes=60 * 1024 * 1024
        ),
    )(tensor, factor_b.T, factor_c)
    return pl.pallas_call(
        finish,
        out_shape=jax.ShapeDtypeStruct((ROWS, R), F32),
        in_specs=[hbm],
        out_specs=vmem,
        scratch_shapes=[
            pltpu.VMEM((M_AT, R), F32),
            pltpu.VMEM((R, R), F32),
            pltpu.VMEM((R, R), F32),
            pltpu.VMEM((R, R), F32),
            dma((2,)),
        ],
        compiler_params=pltpu.CompilerParams(vmem_limit_bytes=60 * 1024 * 1024),
    )(pack)


def solution(mesh):
    return jax.shard_map(
        body,
        mesh=mesh,
        in_specs=(P("ka", "ia", "ja"), P("ja", "ia"), P("ka", "ia")),
        out_specs=P(("ia", "ja", "ka"), None),
        check_vma=False,
    )
```

```python
import jax
import jax.numpy as jnp
from jax import lax
from jax.experimental import pallas as pl
from jax.experimental.pallas import tpu as pltpu
from jax.sharding import PartitionSpec as P

LAMBDA_REG = 0.5
MESH = pl.DeviceIdType.MESH
F32 = jnp.float32
BF16 = jnp.bfloat16
EXACT = lax.Precision.HIGHEST

R = 128
NIA, NJA, NKA = 4, 16, 4
NZ = NJA // 2
RC = R // NIA
KB, IB, JB = 12, 1536, 256
ROWS = IB // (NJA * NKA)
XROWS = 16
BLOCK = ROWS * NKA
PLANE = NIA * NKA
GROWS = R // PLANE
TERMS = 7
R_AT, M_AT, G_AT = ROWS, ROWS + 8, 2 * ROWS + 8
SURE = 2e-4


def nt(a, b):
    return lax.dot_general(a, b, (((1,), (1,)), ((), ())), preferred_element_type=F32)


def tn(a, b):
    return lax.dot_general(a, b, (((0,), (0,)), ((), ())), preferred_element_type=F32)


def exact(a, b):
    return jnp.dot(a, b, preferred_element_type=F32, precision=EXACT)


def eye():
    i = lax.broadcasted_iota(jnp.int32, (R, R), 0)
    j = lax.broadcasted_iota(jnp.int32, (R, R), 1)
    return (i == j).astype(F32)


def split(a):
    high = a.astype(BF16)
    return high, (a - high.astype(F32)).astype(BF16)


def mul3(a, b):
    dot = lambda u, v: jnp.dot(u, v, preferred_element_type=F32)
    return dot(a[0], b[0]) + (dot(a[0], b[1]) + dot(a[1], b[0]))


def fused(
    t_hbm, b_hbm, c_hbm, pack,
    t_v, c_v, cin, gat, bfull, call, gpart, growin, gram,
    psend, precv, own, xin, zown, zin, win, vown, vin,
    t_sem, in_sem, a_send, a_recv, d_send, d_recv, c_send, c_recv, g_send, g_recv, h_send, h_recv,
    p_send, p_recv, x_send, x_recv, z_send, z_recv,
    w_send, w_recv, v_send, v_recv, met_z, met_far, met_plane,
):
    ia, ja, ka = lax.axis_index("ia"), lax.axis_index("ja"), lax.axis_index("ka")
    z, core = ja // 2, lax.rem(ja, 2)
    other = 1 - core
    plane = ia * NKA + ka
    left = []

    def at_y(o):
        return (lax.rem(ia + NIA + o, NIA), ja, ka)

    def at_x(o):
        return (ia, ja, lax.rem(ka + NKA + o, NKA))

    def at_z(o, c=core):
        return (ia, 2 * lax.rem(z + NZ + o, NZ) + c, ka)

    def tell(sem, device):
        pl.semaphore_signal(sem, inc=1, device_id=device, device_id_type=MESH)

    barrier = pltpu.get_barrier_semaphore()
    near = [at_y(o) for o in range(1, NIA)] + [at_z(0, other)]
    near += [at_z(o, c) for o in (1, -1) for c in (core, other)]
    near += [at_x(o) for o in range(1, NKA)]
    for device in near:
        tell(barrier, device)

    load_b = pltpu.make_async_copy(b_hbm, gat.at[ia], in_sem.at[0])
    load_c = pltpu.make_async_copy(c_hbm, c_v, in_sem.at[1])
    load_b.start()
    load_c.start()

    def slab_copy(i, c):
        rows = pl.ds(pl.multiple_of((2 * i + c) * BLOCK, BLOCK), BLOCK)
        return pltpu.make_async_copy(
            t_hbm.at[:, rows], t_v.at[:, rows], t_sem.at[jnp.where(c == other, i, NZ + i)]
        )

    loads = [pltpu.make_async_copy(t_hbm.at[k], t_v.at[k], t_sem.at[k]) for k in range(KB)]
    for load in loads:
        load.start(priority=1)

    pl.semaphore_wait(barrier, len(near))

    def share(source, ref, device, send, recv):
        pltpu.make_async_remote_copy(
            source, ref.at[ia], send, recv, device_id=device, device_id_type=MESH
        ).start()

    for o in (2, 1, 3):
        share(b_hbm, gat, at_y(o), a_send, a_recv)
    for o in (1, -1):
        tell(met_z, at_z(o))
    for o in range(1, NKA):
        tell(met_plane, at_x(o))
    load_c.wait()
    lane = lax.broadcasted_iota(jnp.int32, (KB, R), 1)
    c4 = jnp.concatenate([c_v[...].astype(F32)] * NIA, axis=1)
    cin[ia] = jnp.zeros((16, R), F32)
    cin[ia, 0:KB, :] = jnp.where(lane // RC == ia, c4, 0.0)
    for o in (2, 1, 3):
        share(cin.at[ia], cin, at_y(o), d_send, d_recv)
    pl.semaphore_wait(met_z, 2)
    for o in (2, -2):
        tell(met_far, at_z(o))
    load_b.wait()
    three_b = pltpu.make_async_copy(gat.at[0:3], gat.at[0:3], a_recv)
    three_c = pltpu.make_async_copy(cin.at[0:3], cin.at[0:3], d_recv)
    three_b.wait()
    left.append(pltpu.make_async_copy(gat.at[0:3], gat.at[0:3], a_send).wait)
    left.append(pltpu.make_async_copy(cin.at[0:3], cin.at[0:3], d_send).wait)

    bt = gat[...].reshape(R, JB)
    bfull[...] = bt.astype(F32).T.astype(BF16)
    gpart[...] = nt(bt, bt)
    three_c.wait()
    crows = (cin[0] + cin[1]) + (cin[2] + cin[3])
    call[ka] = crows
    b_all = bfull[...]
    scales = [crows[k : k + 1] for k in range(KB)]

    def contract(rows):
        t = t_v[:, pl.ds(rows, BLOCK), :].reshape(KB * BLOCK, JB)
        products = jnp.dot(t, b_all, preferred_element_type=F32)
        total = products[0:BLOCK] * scales[0]
        for k in range(1, KB):
            total = total + products[k * BLOCK : (k + 1) * BLOCK] * scales[k]
        return total

    def pair_copy(i):
        return pltpu.make_async_remote_copy(
            psend.at[i], precv.at[i], p_send.at[i], p_recv.at[i],
            device_id=(ia, 2 * z + other, ka), device_id_type=MESH,
        )

    def target(t):
        odd = lax.rem(t, 2)
        return lax.rem(z + NZ // 2 + odd * ((t + 1) // 2) - (1 - odd) * (t // 2), NZ)

    def sibling_block(t, carry):
        psend[t] = contract(pl.multiple_of((2 * target(t) + other) * BLOCK, BLOCK))
        pair_copy(t).start()
        return carry

    mine = pl.multiple_of(plane * GROWS, GROWS)
    pl.semaphore_wait(met_far, 2)

    groups = [(o, c) for o in (4, 3, 5, 2, 6, 1, 7) for c in (core, other)] + [(0, other)]
    for slot, (o, c) in enumerate(groups):
        pltpu.make_async_remote_copy(
            gpart.at[pl.ds(mine, GROWS)], growin.at[slot], g_send, g_recv,
            device_id=at_z(o, c), device_id_type=MESH,
        ).start()
    for o in range(1, NKA):
        pltpu.make_async_remote_copy(
            call.at[ka], call.at[ka], c_send, c_recv, device_id=at_x(o), device_id_type=MESH
        ).start()
    left.append(pltpu.make_async_copy(growin, growin, g_send).wait)
    left.append(pltpu.make_async_copy(call.at[0:3], call.at[0:3], c_send).wait)

    for load in loads:
        load.wait()
    lax.fori_loop(0, NZ, sibling_block, 0)
    left.append(lambda: [pair_copy(i).wait_send() for i in range(NZ)])

    def own_block(t, carry):
        to_z = target(t)
        total = contract(pl.multiple_of((2 * to_z + core) * BLOCK, BLOCK))
        pair_copy(t).wait_recv()
        own[to_z] = (total + precv[t]).reshape(NKA, ROWS, R)
        for o in (2, 1, 3):
            to = lax.rem(ka + o, NKA)
            pltpu.make_async_remote_copy(
                own.at[to_z, to, 0:XROWS], xin.at[o - 1, to_z], x_send, x_recv,
                device_id=(ia, ja, to), device_id_type=MESH,
            ).start()

        @pl.when(t < NZ - 1)
        def _():
            pltpu.make_async_remote_copy(
                own.at[to_z, :, XROWS:ROWS], win.at[t], w_send, w_recv,
                device_id=(ia, 2 * to_z + core, ka), device_id_type=MESH,
            ).start()

        return carry

    lax.fori_loop(0, NZ, own_block, 0)
    left.append(pltpu.make_async_copy(xin, xin, x_send).wait)
    left.append(pltpu.make_async_copy(win, win, w_send).wait)

    pltpu.make_async_copy(growin, growin, g_recv).wait()
    rows = gpart[pl.ds(mine, GROWS), :]
    for o in range(NJA - 1):
        rows = rows + growin[o]
    gram[pl.ds(mine, GROWS), :] = rows

    pl.semaphore_wait(met_plane, NKA - 1)
    far_first = lambda o: -(min(o // NKA, NIA - o // NKA) + min(o % NKA, NKA - o % NKA))
    for o in sorted(range(1, PLANE), key=far_first):
        y, x = lax.rem(ia + o // NKA, NIA), lax.rem(ka + o % NKA, NKA)
        pltpu.make_async_remote_copy(
            gram.at[pl.ds(mine, GROWS)], gram.at[pl.ds(mine, GROWS)], h_send, h_recv,
            device_id=(y, ja, x), device_id_type=MESH,
        ).start()
    left.append(pltpu.make_async_copy(gram.at[0 : R - GROWS], gram.at[0 : R - GROWS], h_send).wait)

    pltpu.make_async_copy(xin, xin, x_recv).wait()
    zown[...] = own[:, ka, 0:XROWS, :] + (xin[0] + xin[1] + xin[2])
    for o in (4, 3, 5, 2, 6, 1, 7):
        to = lax.rem(z + o, NZ)
        pltpu.make_async_remote_copy(
            zown.at[to], zin.at[o - 1], z_send, z_recv,
            device_id=(ia, 2 * to + core, ka), device_id_type=MESH,
        ).start()
    left.append(pltpu.make_async_copy(zin, zin, z_send).wait)
    pltpu.make_async_copy(win, win, w_recv).wait()
    rows = own[z, :, XROWS:ROWS, :]
    for t in range(NZ - 1):
        rows = rows + win[t]
    vown[...] = rows
    for o in (2, 1, 3):
        to = lax.rem(ka + o, NKA)
        pltpu.make_async_remote_copy(
            vown.at[to], vin.at[o - 1], v_send, v_recv,
            device_id=(ia, ja, to), device_id_type=MESH,
        ).start()
    left.append(pltpu.make_async_copy(vin, vin, v_send).wait)

    pltpu.make_async_copy(gram.at[0 : R - GROWS], gram.at[0 : R - GROWS], h_recv).wait()
    pltpu.make_async_copy(call.at[0:3], call.at[0:3], c_recv).wait()
    every = call[...].reshape(NKA * 16, R).astype(BF16)
    one = eye()
    g = gram[...] * tn(every, every) + LAMBDA_REG * one
    pack[G_AT:, :] = g
    bound = jnp.max(jnp.sum(jnp.abs(g), axis=0, keepdims=True), axis=1, keepdims=True)
    alpha = 2.0 / (bound + LAMBDA_REG)
    e = one - alpha * g
    p = one + e
    for _ in range(TERMS - 1):
        parts = split(e)
        e = mul3(parts, parts)
        p = p + mul3(split(p), split(e))
    inv = alpha * p
    rest = one - exact(g, inv)
    pack[R_AT : R_AT + 8, :] = jnp.broadcast_to(
        jnp.max(jnp.sum(jnp.abs(rest), axis=0, keepdims=True), axis=1, keepdims=True), (8, R)
    )
    inv = inv + exact(inv, rest)

    pltpu.make_async_copy(vin, vin, v_recv).wait()
    pack[M_AT + XROWS : M_AT + ROWS, :] = vown[ka] + (vin[0] + vin[1] + vin[2])
    pltpu.make_async_copy(zin, zin, z_recv).wait()
    rows = zown[z]
    for o in range(NZ - 1):
        rows = rows + zin[o]
    pack[M_AT : M_AT + XROWS, :] = rows
    pack[0:ROWS, :] = exact(pack[M_AT : M_AT + ROWS, :], inv)
    for wait in left:
        wait()


def finish(pack, out_ref, head, mat, rhs, upper, sem):
    load = pltpu.make_async_copy(pack.at[0:M_AT], head, sem.at[0])
    load.start()
    load.wait()
    sure = jnp.max(head[R_AT:M_AT, :]) < SURE

    @pl.when(sure)
    def _():
        out_ref[...] = head[0:ROWS, :]

    @pl.when(jnp.logical_not(sure))
    def _():
        rhs[...] = jnp.zeros((R, R), F32)
        load_g = pltpu.make_async_copy(pack.at[G_AT:], mat, sem.at[0])
        load_m = pltpu.make_async_copy(pack.at[M_AT:G_AT], rhs.at[0:ROWS], sem.at[1])
        load_g.start()
        load_m.start()
        load_g.wait()
        load_m.wait()
        rhs[...] = rhs[...].T
        down = lax.broadcasted_iota(jnp.int32, (R, 1), 0)
        across = lax.broadcasted_iota(jnp.int32, (1, R), 1)

        def column(a, k):
            return jnp.sum(jnp.where(across == k, a, 0.0), axis=1, keepdims=True)

        def forward(k, carry):
            a = mat[...]
            row = mat[pl.ds(k, 1), :]
            root = jnp.sqrt(jnp.sum(jnp.where(across == k, row, 0.0), axis=1, keepdims=True))
            lrow = jnp.where(across >= k, row / root, 0.0)
            lcol = jnp.where(down > k, column(a, k) / root, 0.0)
            upper[pl.ds(k, 1), :] = lrow
            mat[...] = a - lcol * lrow
            b = rhs[pl.ds(k, 1), :] / root
            rhs[...] = jnp.where(down == k, b, rhs[...] - lcol * b)
            return carry

        lax.fori_loop(0, R, forward, 0)

        def backward(step, carry):
            k = R - 1 - step
            col = column(upper[...], k)
            root = jnp.sum(jnp.where(down == k, col, 0.0), axis=0, keepdims=True)
            x = rhs[pl.ds(k, 1), :] / root
            rhs[...] = jnp.where(
                down == k, x, rhs[...] - jnp.where(down < k, col, 0.0) * x
            )
            return carry

        lax.fori_loop(0, R, backward, 0)
        out_ref[...] = rhs[...].T[0:ROWS]


def body(tensor, factor_b, factor_c):
    vmem = pl.BlockSpec(memory_space=pltpu.VMEM)
    hbm = pl.BlockSpec(memory_space=pltpu.HBM)
    dma, signal = pltpu.SemaphoreType.DMA, pltpu.SemaphoreType.REGULAR
    pack = pl.pallas_call(
        fused,
        out_shape=jax.ShapeDtypeStruct((G_AT + R, R), F32),
        in_specs=[hbm, hbm, hbm],
        out_specs=vmem,
        scratch_shapes=[
            pltpu.VMEM((KB, IB, JB), BF16),
            pltpu.VMEM((KB, RC), BF16),
            pltpu.VMEM((NIA, 16, R), F32),
            pltpu.VMEM((NIA, RC, JB), BF16),
            pltpu.VMEM((JB, R), BF16),
            pltpu.VMEM((NKA, 16, R), F32),
            pltpu.VMEM((R, R), F32),
            pltpu.VMEM((NJA - 1, GROWS, R), F32),
            pltpu.VMEM((R, R), F32),
            pltpu.VMEM((NZ, BLOCK, R), F32),
            pltpu.VMEM((NZ, BLOCK, R), F32),
            pltpu.VMEM((NZ, NKA, ROWS, R), F32),
            pltpu.VMEM((NKA - 1, NZ, XROWS, R), F32),
            pltpu.VMEM((NZ, XROWS, R), F32),
            pltpu.VMEM((NZ - 1, XROWS, R), F32),
            pltpu.VMEM((NZ - 1, NKA, ROWS - XROWS, R), F32),
            pltpu.VMEM((NKA, ROWS - XROWS, R), F32),
            pltpu.VMEM((NKA - 1, ROWS - XROWS, R), F32),
            dma((NJA,)),
            dma((2,)),
            dma, dma, dma, dma, dma, dma, dma, dma, dma, dma,
            dma((NZ,)),
            dma((NZ,)),
            dma, dma, dma, dma, dma, dma, dma, dma,
            signal, signal, signal,
        ],
        compiler_params=pltpu.CompilerParams(
            collective_id=0, has_side_effects=True, vmem_limit_bytes=60 * 1024 * 1024
        ),
    )(tensor, factor_b.T, factor_c)
    return pl.pallas_call(
        finish,
        out_shape=jax.ShapeDtypeStruct((ROWS, R), F32),
        in_specs=[hbm],
        out_specs=vmem,
        scratch_shapes=[
            pltpu.VMEM((M_AT, R), F32),
            pltpu.VMEM((R, R), F32),
            pltpu.VMEM((R, R), F32),
            pltpu.VMEM((R, R), F32),
            dma((2,)),
        ],
        compiler_params=pltpu.CompilerParams(vmem_limit_bytes=60 * 1024 * 1024),
    )(pack)


def solution(mesh):
    return jax.shard_map(
        body,
        mesh=mesh,
        in_specs=(P("ka", "ia", "ja"), P("ja", "ia"), P("ka", "ia")),
        out_specs=P(("ia", "ja", "ka"), None),
        check_vma=False,
    )
```

```python
import jax
import jax.numpy as jnp
from jax import lax
from jax.experimental import pallas as pl
from jax.experimental.pallas import tpu as pltpu
from jax.sharding import PartitionSpec as P

LAMBDA_REG = 0.5
MESH = pl.DeviceIdType.MESH
F32 = jnp.float32
BF16 = jnp.bfloat16
EXACT = lax.Precision.HIGHEST

R = 128
NIA, NJA, NKA = 4, 16, 4
NZ = NJA // 2
RC = R // NIA
KB, IB, JB = 12, 1536, 256
ROWS = IB // (NJA * NKA)
BLOCK = ROWS * NKA
PLANE = NIA * NKA
GROWS = R // PLANE
TERMS = 6
R_AT, M_AT, G_AT = ROWS, ROWS + 8, 2 * ROWS + 8
SURE = 2e-4


def nt(a, b):
    return lax.dot_general(a, b, (((1,), (1,)), ((), ())), preferred_element_type=F32)


def tn(a, b):
    return lax.dot_general(a, b, (((0,), (0,)), ((), ())), preferred_element_type=F32)


def exact(a, b):
    return jnp.dot(a, b, preferred_element_type=F32, precision=EXACT)


def eye():
    i = lax.broadcasted_iota(jnp.int32, (R, R), 0)
    j = lax.broadcasted_iota(jnp.int32, (R, R), 1)
    return (i == j).astype(F32)


def split(a):
    high = a.astype(BF16)
    return high, (a - high.astype(F32)).astype(BF16)


def mul3(a, b):
    dot = lambda u, v: jnp.dot(u, v, preferred_element_type=F32)
    return dot(a[0], b[0]) + (dot(a[0], b[1]) + dot(a[1], b[0]))


def fused(
    t_hbm, bc, pack,
    t_v, gat, bfull, call, gpart, growin, gram,
    psend, precv, own, xin, zown, zin,
    t_sem, in_sem, a_send, a_recv, c_send, c_recv, g_send, g_recv, h_send, h_recv,
    p_send, p_recv, x_send, x_recv, z_send, z_recv, met_z, met_far, met_plane,
):
    ia, ja, ka = lax.axis_index("ia"), lax.axis_index("ja"), lax.axis_index("ka")
    z, core = ja // 2, lax.rem(ja, 2)
    other = 1 - core
    plane = ia * NKA + ka
    left = []

    def at_y(o):
        return (lax.rem(ia + NIA + o, NIA), ja, ka)

    def at_x(o):
        return (ia, ja, lax.rem(ka + NKA + o, NKA))

    def at_z(o, c=core):
        return (ia, 2 * lax.rem(z + NZ + o, NZ) + c, ka)

    def tell(sem, device):
        pl.semaphore_signal(sem, inc=1, device_id=device, device_id_type=MESH)

    def others(me, n):
        return [t + (t >= me).astype(jnp.int32) for t in range(n - 1)]

    keep = pltpu.make_async_copy(bc, gat.at[ia], in_sem)
    keep.start()

    barrier = pltpu.get_barrier_semaphore()
    near = [at_y(o) for o in range(1, NIA)] + [at_z(0, other)]
    near += [at_z(o, c) for o in (1, -1) for c in (core, other)]
    near += [at_x(o) for o in range(1, NKA)]
    for device in near:
        tell(barrier, device)


    def slab_copy(i, c):
        rows = pl.ds(pl.multiple_of((2 * i + c) * BLOCK, BLOCK), BLOCK)
        return pltpu.make_async_copy(
            t_hbm.at[:, rows], t_v.at[:, rows], t_sem.at[jnp.where(c == other, i, NZ + i)]
        )

    loads = [pltpu.make_async_copy(t_hbm.at[k], t_v.at[k], t_sem.at[k]) for k in range(KB)]
    for load in loads:
        load.start(priority=1)

    pl.semaphore_wait(barrier, len(near))
    for y in reversed(others(ia, NIA)):
        pltpu.make_async_remote_copy(
            bc, gat.at[ia], a_send, a_recv, device_id=(y, ja, ka), device_id_type=MESH
        ).start()
    for o in (1, -1):
        tell(met_z, at_z(o))
    for o in range(1, NKA):
        tell(met_plane, at_x(o))
    pl.semaphore_wait(met_z, 2)
    for o in (2, -2):
        tell(met_far, at_z(o))
    keep.wait()
    three = gat.at[0 : NIA - 1]
    pltpu.make_async_copy(three, three, a_recv).wait()
    left.append(pltpu.make_async_copy(three, three, a_send).wait)

    bt = gat[:, 0:RC, :].reshape(R, JB)
    gpart[...] = nt(bt, bt)

    mine = pl.multiple_of(plane * GROWS, GROWS)
    pl.semaphore_wait(met_far, 2)

    growin[ja] = gpart[pl.ds(mine, GROWS), :]
    for to in others(ja, NJA):
        pltpu.make_async_remote_copy(
            growin.at[ja], growin.at[ja], g_send, g_recv,
            device_id=(ia, to, ka), device_id_type=MESH,
        ).start()
    crows = jnp.concatenate([gat[i, RC:, 0:RC].astype(F32) for i in range(NIA)], axis=1)
    call[ka] = crows
    for o in range(1, NKA):
        pltpu.make_async_remote_copy(
            call.at[ka], call.at[ka], c_send, c_recv, device_id=at_x(o), device_id_type=MESH
        ).start()
    left.append(pltpu.make_async_copy(growin.at[1:], growin.at[1:], g_send).wait)
    left.append(pltpu.make_async_copy(call.at[0:3], call.at[0:3], c_send).wait)

    bfull[...] = bt.astype(F32).T.astype(BF16)
    b_all = bfull[...]
    scales = [crows[k : k + 1] for k in range(KB)]

    def contract(rows):
        t = t_v[:, pl.ds(rows, BLOCK), :].reshape(KB * BLOCK, JB)
        products = jnp.dot(t, b_all, preferred_element_type=F32)
        total = products[0:BLOCK] * scales[0]
        for k in range(1, KB):
            total = total + products[k * BLOCK : (k + 1) * BLOCK] * scales[k]
        return total

    def pair_copy(i):
        return pltpu.make_async_remote_copy(
            psend.at[i], precv.at[i], p_send.at[i], p_recv.at[i],
            device_id=(ia, 2 * z + other, ka), device_id_type=MESH,
        )

    def sibling_block(i, carry):
        psend[i] = contract(pl.multiple_of((2 * i + other) * BLOCK, BLOCK))
        pair_copy(i).start()
        return carry

    for load in loads:
        load.wait()
    lax.fori_loop(0, NZ, sibling_block, 0)
    left.append(lambda: [pair_copy(i).wait_send() for i in range(NZ)])

    def own_block(i, carry):
        total = contract(pl.multiple_of((2 * i + core) * BLOCK, BLOCK))
        pair_copy(i).wait_recv()
        own[i] = (total + precv[i]).reshape(NKA, ROWS, R)
        for t, to in enumerate(others(ka, NKA)):
            pltpu.make_async_remote_copy(
                own.at[i, to], xin.at[i, ka - (ka > to).astype(jnp.int32)],
                x_send, x_recv.at[i], device_id=(ia, ja, to), device_id_type=MESH,
            ).start()
        return carry

    lax.fori_loop(0, NZ, own_block, 0)
    left.append(pltpu.make_async_copy(xin, xin, x_send).wait)

    def forward(i, carry):
        pltpu.make_async_copy(xin.at[i], xin.at[i], x_recv.at[i]).wait()
        zown[i] = own[i, ka] + (xin[i, 0] + xin[i, 1] + xin[i, 2])

        @pl.when(i != z)
        def _():
            pltpu.make_async_remote_copy(
                zown.at[i], zin.at[z], z_send, z_recv,
                device_id=(ia, 2 * i + core, ka), device_id_type=MESH,
            ).start()

        return carry

    pltpu.make_async_copy(growin.at[1:], growin.at[1:], g_recv).wait()
    rows = growin[0]
    for o in range(1, NJA):
        rows = rows + growin[o]
    gram[pl.ds(mine, GROWS), :] = rows
    pl.semaphore_wait(met_plane, NKA - 1)
    for p in others(plane, PLANE):
        pltpu.make_async_remote_copy(
            gram.at[pl.ds(mine, GROWS)], gram.at[pl.ds(mine, GROWS)], h_send, h_recv,
            device_id=(p // NKA, ja, lax.rem(p, NKA)), device_id_type=MESH,
        ).start()
    left.append(pltpu.make_async_copy(gram.at[0 : R - GROWS], gram.at[0 : R - GROWS], h_send).wait)
    lax.fori_loop(0, NZ, forward, 0)
    left.append(pltpu.make_async_copy(zin.at[1:], zin.at[1:], z_send).wait)

    pltpu.make_async_copy(gram.at[0 : R - GROWS], gram.at[0 : R - GROWS], h_recv).wait()
    pltpu.make_async_copy(call.at[0:3], call.at[0:3], c_recv).wait()
    every = call[...].reshape(NKA * 16, R).astype(BF16)
    one = eye()
    g = gram[...] * tn(every, every) + LAMBDA_REG * one
    pack[G_AT:, :] = g
    bound = jnp.max(jnp.sum(jnp.abs(g), axis=0, keepdims=True), axis=1, keepdims=True)
    alpha = 1.75 / bound
    e = one - alpha * g
    p = one + e
    for _ in range(TERMS - 1):
        parts = split(e)
        e = mul3(parts, parts)
        p = p + mul3(split(p), split(e))
    inv = alpha * p
    rest = one - exact(g, inv)
    pack[R_AT : R_AT + 8, :] = jnp.broadcast_to(
        jnp.max(jnp.sum(jnp.abs(rest), axis=0, keepdims=True), axis=1, keepdims=True), (8, R)
    )
    inv = inv + mul3(split(inv), split(rest))

    zin[z] = zown[z]
    pltpu.make_async_copy(zin.at[1:], zin.at[1:], z_recv).wait()
    rows = zin[0]
    for o in range(1, NZ):
        rows = rows + zin[o]
    pack[M_AT : M_AT + ROWS, :] = rows
    pack[0:ROWS, :] = exact(rows, inv)
    for wait in left:
        wait()


def finish(pack, out_ref, head, mat, rhs, upper, sem):
    load = pltpu.make_async_copy(pack.at[0:M_AT], head, sem.at[0])
    load.start()
    load.wait()
    sure = jnp.max(head[R_AT:M_AT, :]) < SURE

    @pl.when(sure)
    def _():
        out_ref[...] = head[0:ROWS, :]

    @pl.when(jnp.logical_not(sure))
    def _():
        rhs[...] = jnp.zeros((R, R), F32)
        load_g = pltpu.make_async_copy(pack.at[G_AT:], mat, sem.at[0])
        load_m = pltpu.make_async_copy(pack.at[M_AT:G_AT], rhs.at[0:ROWS], sem.at[1])
        load_g.start()
        load_m.start()
        load_g.wait()
        load_m.wait()
        rhs[...] = rhs[...].T
        down = lax.broadcasted_iota(jnp.int32, (R, 1), 0)
        across = lax.broadcasted_iota(jnp.int32, (1, R), 1)

        def column(a, k):
            return jnp.sum(jnp.where(across == k, a, 0.0), axis=1, keepdims=True)

        def forward(k, carry):
            a = mat[...]
            row = mat[pl.ds(k, 1), :]
            root = jnp.sqrt(jnp.sum(jnp.where(across == k, row, 0.0), axis=1, keepdims=True))
            lrow = jnp.where(across >= k, row / root, 0.0)
            lcol = jnp.where(down > k, column(a, k) / root, 0.0)
            upper[pl.ds(k, 1), :] = lrow
            mat[...] = a - lcol * lrow
            b = rhs[pl.ds(k, 1), :] / root
            rhs[...] = jnp.where(down == k, b, rhs[...] - lcol * b)
            return carry

        lax.fori_loop(0, R, forward, 0)

        def backward(step, carry):
            k = R - 1 - step
            col = column(upper[...], k)
            root = jnp.sum(jnp.where(down == k, col, 0.0), axis=0, keepdims=True)
            x = rhs[pl.ds(k, 1), :] / root
            rhs[...] = jnp.where(
                down == k, x, rhs[...] - jnp.where(down < k, col, 0.0) * x
            )
            return carry

        lax.fori_loop(0, R, backward, 0)
        out_ref[...] = rhs[...].T[0:ROWS]


def body(tensor, factor_b, factor_c):
    vmem = pl.BlockSpec(memory_space=pltpu.VMEM)
    hbm = pl.BlockSpec(memory_space=pltpu.HBM)
    dma, signal = pltpu.SemaphoreType.DMA, pltpu.SemaphoreType.REGULAR
    c_rows = jnp.pad(factor_c, ((0, 16 - KB), (0, JB - RC)))
    both = jnp.concatenate([factor_b.T, c_rows], axis=0)
    pack = pl.pallas_call(
        fused,
        out_shape=jax.ShapeDtypeStruct((G_AT + R, R), F32),
        in_specs=[hbm, pl.BlockSpec(memory_space=pl.ANY)],
        out_specs=vmem,
        scratch_shapes=[
            pltpu.VMEM((KB, IB, JB), BF16),
            pltpu.VMEM((NIA, RC + 16, JB), BF16),
            pltpu.VMEM((JB, R), BF16),
            pltpu.VMEM((NKA, 16, R), F32),
            pltpu.VMEM((R, R), F32),
            pltpu.VMEM((NJA, GROWS, R), F32),
            pltpu.VMEM((R, R), F32),
            pltpu.VMEM((NZ, BLOCK, R), F32),
            pltpu.VMEM((NZ, BLOCK, R), F32),
            pltpu.VMEM((NZ, NKA, ROWS, R), F32),
            pltpu.VMEM((NZ, NKA - 1, ROWS, R), F32),
            pltpu.VMEM((NZ, ROWS, R), F32),
            pltpu.VMEM((NZ, ROWS, R), F32),
            dma((NJA,)),
            dma, dma, dma, dma, dma, dma, dma, dma, dma,
            dma((NZ,)),
            dma((NZ,)),
            dma,
            dma((NZ,)),
            dma, dma,
            signal, signal, signal,
        ],
        compiler_params=pltpu.CompilerParams(
            collective_id=0, has_side_effects=True, vmem_limit_bytes=52 * 1024 * 1024
        ),
    )(tensor, both)
    return pl.pallas_call(
        finish,
        out_shape=jax.ShapeDtypeStruct((ROWS, R), F32),
        in_specs=[hbm],
        out_specs=vmem,
        scratch_shapes=[
            pltpu.VMEM((M_AT, R), F32),
            pltpu.VMEM((R, R), F32),
            pltpu.VMEM((R, R), F32),
            pltpu.VMEM((R, R), F32),
            dma((2,)),
        ],
        compiler_params=pltpu.CompilerParams(vmem_limit_bytes=8 * 1024 * 1024),
    )(pack)


def solution(mesh):
    return jax.shard_map(
        body,
        mesh=mesh,
        in_specs=(P("ka", "ia", "ja"), P("ja", "ia"), P("ka", "ia")),
        out_specs=P(("ia", "ja", "ka"), None),
        check_vma=False,
    )
```

```python
import jax
import jax.numpy as jnp
from jax import lax
from jax.experimental import pallas as pl
from jax.experimental.pallas import tpu as pltpu
from jax.sharding import PartitionSpec as P

LAMBDA_REG = 0.5
MESH = pl.DeviceIdType.MESH
F32 = jnp.float32
BF16 = jnp.bfloat16
EXACT = lax.Precision.HIGHEST

R = 128
NIA, NJA, NKA = 4, 16, 4
NZ = NJA // 2
RC = R // NIA
KB, IB, JB = 12, 1536, 256
ROWS = IB // (NJA * NKA)
BLOCK = ROWS * NKA
PLANE = NIA * NKA
GROWS = R // PLANE
TERMS = 8
R_AT, M_AT, G_AT = ROWS, ROWS + 8, 2 * ROWS + 8
SURE = 2e-4


def nt(a, b):
    return lax.dot_general(a, b, (((1,), (1,)), ((), ())), preferred_element_type=F32)


def tn(a, b):
    return lax.dot_general(a, b, (((0,), (0,)), ((), ())), preferred_element_type=F32)


def exact(a, b):
    return jnp.dot(a, b, preferred_element_type=F32, precision=EXACT)


def eye():
    i = lax.broadcasted_iota(jnp.int32, (R, R), 0)
    j = lax.broadcasted_iota(jnp.int32, (R, R), 1)
    return (i == j).astype(F32)


def split(a):
    high = a.astype(BF16)
    return high, (a - high.astype(F32)).astype(BF16)


def mul3(a, b):
    dot = lambda u, v: jnp.dot(u, v, preferred_element_type=F32)
    return dot(a[0], b[0]) + (dot(a[0], b[1]) + dot(a[1], b[0]))


def fused(
    t_hbm, bc, pack,
    t_v, gat, bfull, call, gpart, growin, gram,
    psend, precv, own, xin, zown, zin,
    t_sem, in_sem, a_send, a_recv, c_send, c_recv, g_send, g_recv, h_send, h_recv,
    p_send, p_recv, x_send, x_recv, z_send, z_recv, met_z, met_far, met_plane,
):
    ia, ja, ka = lax.axis_index("ia"), lax.axis_index("ja"), lax.axis_index("ka")
    z, core = ja // 2, lax.rem(ja, 2)
    other = 1 - core
    plane = ia * NKA + ka
    left = []

    def at_y(o):
        return (lax.rem(ia + NIA + o, NIA), ja, ka)

    def at_x(o):
        return (ia, ja, lax.rem(ka + NKA + o, NKA))

    def at_z(o, c=core):
        return (ia, 2 * lax.rem(z + NZ + o, NZ) + c, ka)

    def tell(sem, device):
        pl.semaphore_signal(sem, inc=1, device_id=device, device_id_type=MESH)

    def others(me, n):
        return [t + (t >= me).astype(jnp.int32) for t in range(n - 1)]

    keep = pltpu.make_async_copy(bc, gat.at[ia], in_sem)
    keep.start()

    barrier = pltpu.get_barrier_semaphore()
    near = [at_y(o) for o in range(1, NIA)] + [at_z(0, other)]
    near += [at_z(o, c) for o in (1, -1) for c in (core, other)]
    near += [at_x(o) for o in range(1, NKA)]
    for device in near:
        tell(barrier, device)


    def slab_copy(i, c):
        rows = pl.ds(pl.multiple_of((2 * i + c) * BLOCK, BLOCK), BLOCK)
        return pltpu.make_async_copy(
            t_hbm.at[:, rows], t_v.at[:, rows], t_sem.at[jnp.where(c == other, i, NZ + i)]
        )

    loads = [pltpu.make_async_copy(t_hbm.at[k], t_v.at[k], t_sem.at[k]) for k in range(KB)]
    for load in loads:
        load.start(priority=1)

    pl.semaphore_wait(barrier, len(near))
    for y in reversed(others(ia, NIA)):
        pltpu.make_async_remote_copy(
            bc, gat.at[ia], a_send, a_recv, device_id=(y, ja, ka), device_id_type=MESH
        ).start()
    for o in (1, -1):
        tell(met_z, at_z(o))
    for o in range(1, NKA):
        tell(met_plane, at_x(o))
    pl.semaphore_wait(met_z, 2)
    for o in (2, -2):
        tell(met_far, at_z(o))
    keep.wait()
    three = gat.at[0 : NIA - 1]
    pltpu.make_async_copy(three, three, a_recv).wait()
    left.append(pltpu.make_async_copy(three, three, a_send).wait)

    bt = gat[:, 0:RC, :].reshape(R, JB)
    gpart[...] = nt(bt, bt)

    mine = pl.multiple_of(plane * GROWS, GROWS)
    pl.semaphore_wait(met_far, 2)

    growin[ja] = gpart[pl.ds(mine, GROWS), :]
    for to in others(ja, NJA):
        pltpu.make_async_remote_copy(
            growin.at[ja], growin.at[ja], g_send, g_recv,
            device_id=(ia, to, ka), device_id_type=MESH,
        ).start()
    crows = jnp.concatenate([gat[i, RC:, 0:RC].astype(F32) for i in range(NIA)], axis=1)
    call[ka] = crows
    for o in range(1, NKA):
        pltpu.make_async_remote_copy(
            call.at[ka], call.at[ka], c_send, c_recv, device_id=at_x(o), device_id_type=MESH
        ).start()
    left.append(pltpu.make_async_copy(growin.at[1:], growin.at[1:], g_send).wait)
    left.append(pltpu.make_async_copy(call.at[0:3], call.at[0:3], c_send).wait)

    bfull[...] = bt.astype(F32).T.astype(BF16)
    b_all = bfull[...]
    scales = [crows[k : k + 1] for k in range(KB)]

    def contract(rows):
        t = t_v[:, pl.ds(rows, BLOCK), :].reshape(KB * BLOCK, JB)
        products = jnp.dot(t, b_all, preferred_element_type=F32)
        total = products[0:BLOCK] * scales[0]
        for k in range(1, KB):
            total = total + products[k * BLOCK : (k + 1) * BLOCK] * scales[k]
        return total

    def pair_copy(i):
        return pltpu.make_async_remote_copy(
            psend.at[i], precv.at[i], p_send.at[i], p_recv.at[i],
            device_id=(ia, 2 * z + other, ka), device_id_type=MESH,
        )

    def sibling_block(i, carry):
        psend[i] = contract(pl.multiple_of((2 * i + other) * BLOCK, BLOCK))
        pair_copy(i).start()
        return carry

    for load in loads:
        load.wait()
    lax.fori_loop(0, NZ, sibling_block, 0)
    left.append(lambda: [pair_copy(i).wait_send() for i in range(NZ)])

    def own_block(i, carry):
        total = contract(pl.multiple_of((2 * i + core) * BLOCK, BLOCK))
        pair_copy(i).wait_recv()
        own[i] = (total + precv[i]).reshape(NKA, ROWS, R)
        for t, to in enumerate(others(ka, NKA)):
            pltpu.make_async_remote_copy(
                own.at[i, to], xin.at[i, ka - (ka > to).astype(jnp.int32)],
                x_send, x_recv.at[i], device_id=(ia, ja, to), device_id_type=MESH,
            ).start()
        return carry

    lax.fori_loop(0, NZ, own_block, 0)
    left.append(pltpu.make_async_copy(xin, xin, x_send).wait)

    def forward(i, carry):
        pltpu.make_async_copy(xin.at[i], xin.at[i], x_recv.at[i]).wait()
        zown[i] = own[i, ka] + (xin[i, 0] + xin[i, 1] + xin[i, 2])

        @pl.when(i != z)
        def _():
            pltpu.make_async_remote_copy(
                zown.at[i], zin.at[z], z_send, z_recv,
                device_id=(ia, 2 * i + core, ka), device_id_type=MESH,
            ).start()

        return carry

    pltpu.make_async_copy(growin.at[1:], growin.at[1:], g_recv).wait()
    rows = growin[0]
    for o in range(1, NJA):
        rows = rows + growin[o]
    gram[pl.ds(mine, GROWS), :] = rows
    pl.semaphore_wait(met_plane, NKA - 1)
    for p in others(plane, PLANE):
        pltpu.make_async_remote_copy(
            gram.at[pl.ds(mine, GROWS)], gram.at[pl.ds(mine, GROWS)], h_send, h_recv,
            device_id=(p // NKA, ja, lax.rem(p, NKA)), device_id_type=MESH,
        ).start()
    left.append(pltpu.make_async_copy(gram.at[0 : R - GROWS], gram.at[0 : R - GROWS], h_send).wait)
    lax.fori_loop(0, NZ, forward, 0)
    left.append(pltpu.make_async_copy(zin.at[1:], zin.at[1:], z_send).wait)

    pltpu.make_async_copy(gram.at[0 : R - GROWS], gram.at[0 : R - GROWS], h_recv).wait()
    pltpu.make_async_copy(call.at[0:3], call.at[0:3], c_recv).wait()
    every = call[...].reshape(NKA * 16, R).astype(BF16)
    one = eye()
    g = gram[...] * tn(every, every) + LAMBDA_REG * one
    pack[G_AT:, :] = g
    bound = jnp.max(jnp.sum(jnp.abs(g), axis=0, keepdims=True), axis=1, keepdims=True)
    alpha = 2.0 / (bound + LAMBDA_REG)
    e = one - alpha * g
    p = one + e
    for _ in range(TERMS - 1):
        parts = split(e)
        e = mul3(parts, parts)
        p = p + mul3(split(p), split(e))
    inv = alpha * p
    rest = one - exact(g, inv)
    pack[R_AT : R_AT + 8, :] = jnp.broadcast_to(
        jnp.max(jnp.sum(jnp.abs(rest), axis=0, keepdims=True), axis=1, keepdims=True), (8, R)
    )
    inv = inv + mul3(split(inv), split(rest))

    zin[z] = zown[z]
    pltpu.make_async_copy(zin.at[1:], zin.at[1:], z_recv).wait()
    rows = zin[0]
    for o in range(1, NZ):
        rows = rows + zin[o]
    pack[M_AT : M_AT + ROWS, :] = rows
    pack[0:ROWS, :] = exact(rows, inv)
    for wait in left:
        wait()


def finish(pack, out_ref, head, mat, rhs, upper, sem):
    load = pltpu.make_async_copy(pack.at[0:M_AT], head, sem.at[0])
    load.start()
    load.wait()
    sure = jnp.max(head[R_AT:M_AT, :]) < SURE

    @pl.when(sure)
    def _():
        out_ref[...] = head[0:ROWS, :]

    @pl.when(jnp.logical_not(sure))
    def _():
        rhs[...] = jnp.zeros((R, R), F32)
        load_g = pltpu.make_async_copy(pack.at[G_AT:], mat, sem.at[0])
        load_m = pltpu.make_async_copy(pack.at[M_AT:G_AT], rhs.at[0:ROWS], sem.at[1])
        load_g.start()
        load_m.start()
        load_g.wait()
        load_m.wait()
        rhs[...] = rhs[...].T
        down = lax.broadcasted_iota(jnp.int32, (R, 1), 0)
        across = lax.broadcasted_iota(jnp.int32, (1, R), 1)

        def column(a, k):
            return jnp.sum(jnp.where(across == k, a, 0.0), axis=1, keepdims=True)

        def forward(k, carry):
            a = mat[...]
            row = mat[pl.ds(k, 1), :]
            root = jnp.sqrt(jnp.sum(jnp.where(across == k, row, 0.0), axis=1, keepdims=True))
            lrow = jnp.where(across >= k, row / root, 0.0)
            lcol = jnp.where(down > k, column(a, k) / root, 0.0)
            upper[pl.ds(k, 1), :] = lrow
            mat[...] = a - lcol * lrow
            b = rhs[pl.ds(k, 1), :] / root
            rhs[...] = jnp.where(down == k, b, rhs[...] - lcol * b)
            return carry

        lax.fori_loop(0, R, forward, 0)

        def backward(step, carry):
            k = R - 1 - step
            col = column(upper[...], k)
            root = jnp.sum(jnp.where(down == k, col, 0.0), axis=0, keepdims=True)
            x = rhs[pl.ds(k, 1), :] / root
            rhs[...] = jnp.where(
                down == k, x, rhs[...] - jnp.where(down < k, col, 0.0) * x
            )
            return carry

        lax.fori_loop(0, R, backward, 0)
        out_ref[...] = rhs[...].T[0:ROWS]


def body(tensor, factor_b, factor_c):
    vmem = pl.BlockSpec(memory_space=pltpu.VMEM)
    hbm = pl.BlockSpec(memory_space=pltpu.HBM)
    dma, signal = pltpu.SemaphoreType.DMA, pltpu.SemaphoreType.REGULAR
    c_rows = jnp.pad(factor_c, ((0, 16 - KB), (0, JB - RC)))
    both = jnp.concatenate([factor_b.T, c_rows], axis=0)
    pack = pl.pallas_call(
        fused,
        out_shape=jax.ShapeDtypeStruct((G_AT + R, R), F32),
        in_specs=[hbm, pl.BlockSpec(memory_space=pl.ANY)],
        out_specs=vmem,
        scratch_shapes=[
            pltpu.VMEM((KB, IB, JB), BF16),
            pltpu.VMEM((NIA, RC + 16, JB), BF16),
            pltpu.VMEM((JB, R), BF16),
            pltpu.VMEM((NKA, 16, R), F32),
            pltpu.VMEM((R, R), F32),
            pltpu.VMEM((NJA, GROWS, R), F32),
            pltpu.VMEM((R, R), F32),
            pltpu.VMEM((NZ, BLOCK, R), F32),
            pltpu.VMEM((NZ, BLOCK, R), F32),
            pltpu.VMEM((NZ, NKA, ROWS, R), F32),
            pltpu.VMEM((NZ, NKA - 1, ROWS, R), F32),
            pltpu.VMEM((NZ, ROWS, R), F32),
            pltpu.VMEM((NZ, ROWS, R), F32),
            dma((NJA,)),
            dma, dma, dma, dma, dma, dma, dma, dma, dma,
            dma((NZ,)),
            dma((NZ,)),
            dma,
            dma((NZ,)),
            dma, dma,
            signal, signal, signal,
        ],
        compiler_params=pltpu.CompilerParams(
            collective_id=0, has_side_effects=True, vmem_limit_bytes=52 * 1024 * 1024
        ),
    )(tensor, both)
    return pl.pallas_call(
        finish,
        out_shape=jax.ShapeDtypeStruct((ROWS, R), F32),
        in_specs=[hbm],
        out_specs=vmem,
        scratch_shapes=[
            pltpu.VMEM((M_AT, R), F32),
            pltpu.VMEM((R, R), F32),
            pltpu.VMEM((R, R), F32),
            pltpu.VMEM((R, R), F32),
            dma((2,)),
        ],
        compiler_params=pltpu.CompilerParams(vmem_limit_bytes=8 * 1024 * 1024),
    )(pack)


def solution(mesh):
    return jax.shard_map(
        body,
        mesh=mesh,
        in_specs=(P("ka", "ia", "ja"), P("ja", "ia"), P("ka", "ia")),
        out_specs=P(("ia", "ja", "ka"), None),
        check_vma=False,
    )
```

```python
import jax
import jax.numpy as jnp
from jax import lax
from jax.experimental import pallas as pl
from jax.experimental.pallas import tpu as pltpu
from jax.sharding import PartitionSpec as P

LAMBDA_REG = 0.5
MESH = pl.DeviceIdType.MESH
F32 = jnp.float32
BF16 = jnp.bfloat16
EXACT = lax.Precision.HIGHEST

R = 128
NIA, NJA, NKA = 4, 16, 4
NZ = NJA // 2
RC = R // NIA
KB, IB, JB = 12, 1536, 256
ROWS = IB // (NJA * NKA)
BLOCK = ROWS * NKA
PLANE = NIA * NKA
GROWS = R // PLANE
TERMS = 7
R_AT, M_AT, G_AT = ROWS, ROWS + 8, 2 * ROWS + 8
SURE = 2e-4


def nt(a, b):
    return lax.dot_general(a, b, (((1,), (1,)), ((), ())), preferred_element_type=F32)


def tn(a, b):
    return lax.dot_general(a, b, (((0,), (0,)), ((), ())), preferred_element_type=F32)


def exact(a, b):
    return jnp.dot(a, b, preferred_element_type=F32, precision=EXACT)


def eye():
    i = lax.broadcasted_iota(jnp.int32, (R, R), 0)
    j = lax.broadcasted_iota(jnp.int32, (R, R), 1)
    return (i == j).astype(F32)


def split(a):
    high = a.astype(BF16)
    return high, (a - high.astype(F32)).astype(BF16)


def mul3(a, b):
    both = jnp.concatenate(a, axis=1)
    twice = jnp.concatenate([b[0], b[0]], axis=0)
    return jnp.dot(both, twice, preferred_element_type=F32) + jnp.dot(
        a[0], b[1], preferred_element_type=F32
    )


def fused(
    t_hbm, bc, pack,
    t_v, gat, bfull, call, gpart, growin, gram,
    psend, precv, own, xin, zown, zin,
    t_sem, in_sem, a_send, a_recv, c_send, c_recv, g_send, g_recv, h_send, h_recv,
    p_send, p_recv, x_send, x_recv, z_send, z_recv, met_z, met_far, met_plane,
):
    ia, ja, ka = lax.axis_index("ia"), lax.axis_index("ja"), lax.axis_index("ka")
    z, core = ja // 2, lax.rem(ja, 2)
    other = 1 - core
    plane = ia * NKA + ka
    left = []

    def at_y(o):
        return (lax.rem(ia + NIA + o, NIA), ja, ka)

    def at_x(o):
        return (ia, ja, lax.rem(ka + NKA + o, NKA))

    def at_z(o, c=core):
        return (ia, 2 * lax.rem(z + NZ + o, NZ) + c, ka)

    def tell(sem, device):
        pl.semaphore_signal(sem, inc=1, device_id=device, device_id_type=MESH)

    def others(me, n):
        return [t + (t >= me).astype(jnp.int32) for t in range(n - 1)]

    keep = pltpu.make_async_copy(bc, gat.at[ia], in_sem)
    keep.start()

    barrier = pltpu.get_barrier_semaphore()
    near = [at_y(o) for o in range(1, NIA)] + [at_z(0, other)]
    near += [at_z(o, c) for o in (1, -1) for c in (core, other)]
    near += [at_x(o) for o in range(1, NKA)]
    for device in near:
        tell(barrier, device)


    def slab_copy(i, c):
        rows = pl.ds(pl.multiple_of((2 * i + c) * BLOCK, BLOCK), BLOCK)
        return pltpu.make_async_copy(
            t_hbm.at[:, rows], t_v.at[:, rows], t_sem.at[jnp.where(c == other, i, NZ + i)]
        )

    loads = [pltpu.make_async_copy(t_hbm.at[k], t_v.at[k], t_sem.at[k]) for k in range(KB)]
    for load in loads:
        load.start(priority=1)

    pl.semaphore_wait(barrier, len(near))
    for y in reversed(others(ia, NIA)):
        pltpu.make_async_remote_copy(
            bc, gat.at[ia], a_send, a_recv, device_id=(y, ja, ka), device_id_type=MESH
        ).start()
    for o in (1, -1):
        tell(met_z, at_z(o))
    for o in range(1, NKA):
        tell(met_plane, at_x(o))
    pl.semaphore_wait(met_z, 2)
    for o in (2, -2):
        tell(met_far, at_z(o))
    keep.wait()
    three = gat.at[0 : NIA - 1]
    pltpu.make_async_copy(three, three, a_recv).wait()
    left.append(pltpu.make_async_copy(three, three, a_send).wait)

    bt = gat[:, 0:RC, :].reshape(R, JB)
    gpart[...] = nt(bt, bt)

    mine = pl.multiple_of(plane * GROWS, GROWS)
    pl.semaphore_wait(met_far, 2)

    growin[ja] = gpart[pl.ds(mine, GROWS), :]
    for to in others(ja, NJA):
        pltpu.make_async_remote_copy(
            growin.at[ja], growin.at[ja], g_send, g_recv,
            device_id=(ia, to, ka), device_id_type=MESH,
        ).start()
    crows = jnp.concatenate([gat[i, RC:, 0:RC].astype(F32) for i in range(NIA)], axis=1)
    call[ka] = crows
    for o in range(1, NKA):
        pltpu.make_async_remote_copy(
            call.at[ka], call.at[ka], c_send, c_recv, device_id=at_x(o), device_id_type=MESH
        ).start()
    left.append(pltpu.make_async_copy(growin.at[1:], growin.at[1:], g_send).wait)
    left.append(pltpu.make_async_copy(call.at[0:3], call.at[0:3], c_send).wait)

    bfull[...] = bt.astype(F32).T.astype(BF16)
    b_all = bfull[...]
    scales = [crows[k : k + 1] for k in range(KB)]

    def contract(rows):
        t = t_v[:, pl.ds(rows, BLOCK), :].reshape(KB * BLOCK, JB)
        products = jnp.dot(t, b_all, preferred_element_type=F32)
        total = products[0:BLOCK] * scales[0]
        for k in range(1, KB):
            total = total + products[k * BLOCK : (k + 1) * BLOCK] * scales[k]
        return total

    def pair_copy(i):
        return pltpu.make_async_remote_copy(
            psend.at[i], precv.at[i], p_send.at[i], p_recv.at[i],
            device_id=(ia, 2 * z + other, ka), device_id_type=MESH,
        )

    def sibling_block(i, carry):
        psend[i] = contract(pl.multiple_of((2 * i + other) * BLOCK, BLOCK))
        pair_copy(i).start()
        return carry

    for load in loads:
        load.wait()
    lax.fori_loop(0, NZ, sibling_block, 0)
    left.append(lambda: [pair_copy(i).wait_send() for i in range(NZ)])

    def own_block(i, carry):
        total = contract(pl.multiple_of((2 * i + core) * BLOCK, BLOCK))
        pair_copy(i).wait_recv()
        own[i] = (total + precv[i]).reshape(NKA, ROWS, R)
        for t, to in enumerate(others(ka, NKA)):
            pltpu.make_async_remote_copy(
                own.at[i, to], xin.at[i, ka - (ka > to).astype(jnp.int32)],
                x_send, x_recv.at[i], device_id=(ia, ja, to), device_id_type=MESH,
            ).start()
        return carry

    lax.fori_loop(0, NZ, own_block, 0)
    left.append(pltpu.make_async_copy(xin, xin, x_send).wait)

    def forward(i, carry):
        pltpu.make_async_copy(xin.at[i], xin.at[i], x_recv.at[i]).wait()
        zown[i] = own[i, ka] + (xin[i, 0] + xin[i, 1] + xin[i, 2])

        @pl.when(i != z)
        def _():
            pltpu.make_async_remote_copy(
                zown.at[i], zin.at[z], z_send, z_recv,
                device_id=(ia, 2 * i + core, ka), device_id_type=MESH,
            ).start()

        return carry

    pltpu.make_async_copy(growin.at[1:], growin.at[1:], g_recv).wait()
    rows = growin[0]
    for o in range(1, NJA):
        rows = rows + growin[o]
    gram[pl.ds(mine, GROWS), :] = rows
    pl.semaphore_wait(met_plane, NKA - 1)
    for p in others(plane, PLANE):
        pltpu.make_async_remote_copy(
            gram.at[pl.ds(mine, GROWS)], gram.at[pl.ds(mine, GROWS)], h_send, h_recv,
            device_id=(p // NKA, ja, lax.rem(p, NKA)), device_id_type=MESH,
        ).start()
    left.append(pltpu.make_async_copy(gram.at[0 : R - GROWS], gram.at[0 : R - GROWS], h_send).wait)
    lax.fori_loop(0, NZ, forward, 0)
    left.append(pltpu.make_async_copy(zin.at[1:], zin.at[1:], z_send).wait)

    pltpu.make_async_copy(gram.at[0 : R - GROWS], gram.at[0 : R - GROWS], h_recv).wait()
    pltpu.make_async_copy(call.at[0:3], call.at[0:3], c_recv).wait()
    every = call[...].reshape(NKA * 16, R).astype(BF16)
    one = eye()
    g = gram[...] * tn(every, every) + LAMBDA_REG * one
    pack[G_AT:, :] = g
    size = jnp.abs(g)
    across = jnp.sum(size, axis=0, keepdims=True)
    down = jnp.sum(size, axis=1, keepdims=True)
    bound = jnp.max(jnp.sum(size * across, axis=1, keepdims=True) / down, axis=0, keepdims=True)
    alpha = 2.0 / (bound + LAMBDA_REG)
    e = one - alpha * g
    p = one + e
    for _ in range(TERMS - 1):
        parts = split(e)
        e = mul3(parts, parts)
        p = p + mul3(split(p), split(e))
    inv = alpha * p
    rest = one - exact(g, inv)
    pack[R_AT : R_AT + 8, :] = jnp.broadcast_to(
        jnp.max(jnp.sum(jnp.abs(rest), axis=0, keepdims=True), axis=1, keepdims=True), (8, R)
    )
    inv = inv + mul3(split(inv), split(rest))

    zin[z] = zown[z]
    pltpu.make_async_copy(zin.at[1:], zin.at[1:], z_recv).wait()
    rows = zin[0]
    for o in range(1, NZ):
        rows = rows + zin[o]
    pack[M_AT : M_AT + ROWS, :] = rows
    pack[0:ROWS, :] = exact(rows, inv)
    for wait in left:
        wait()


def finish(pack, out_ref, head, mat, rhs, upper, sem):
    load = pltpu.make_async_copy(pack.at[0:M_AT], head, sem.at[0])
    load.start()
    load.wait()
    sure = jnp.max(head[R_AT:M_AT, :]) < SURE

    @pl.when(sure)
    def _():
        out_ref[...] = head[0:ROWS, :]

    @pl.when(jnp.logical_not(sure))
    def _():
        rhs[...] = jnp.zeros((R, R), F32)
        load_g = pltpu.make_async_copy(pack.at[G_AT:], mat, sem.at[0])
        load_m = pltpu.make_async_copy(pack.at[M_AT:G_AT], rhs.at[0:ROWS], sem.at[1])
        load_g.start()
        load_m.start()
        load_g.wait()
        load_m.wait()
        rhs[...] = rhs[...].T
        down = lax.broadcasted_iota(jnp.int32, (R, 1), 0)
        across = lax.broadcasted_iota(jnp.int32, (1, R), 1)

        def column(a, k):
            return jnp.sum(jnp.where(across == k, a, 0.0), axis=1, keepdims=True)

        def forward(k, carry):
            a = mat[...]
            row = mat[pl.ds(k, 1), :]
            root = jnp.sqrt(jnp.sum(jnp.where(across == k, row, 0.0), axis=1, keepdims=True))
            lrow = jnp.where(across >= k, row / root, 0.0)
            lcol = jnp.where(down > k, column(a, k) / root, 0.0)
            upper[pl.ds(k, 1), :] = lrow
            mat[...] = a - lcol * lrow
            b = rhs[pl.ds(k, 1), :] / root
            rhs[...] = jnp.where(down == k, b, rhs[...] - lcol * b)
            return carry

        lax.fori_loop(0, R, forward, 0)

        def backward(step, carry):
            k = R - 1 - step
            col = column(upper[...], k)
            root = jnp.sum(jnp.where(down == k, col, 0.0), axis=0, keepdims=True)
            x = rhs[pl.ds(k, 1), :] / root
            rhs[...] = jnp.where(
                down == k, x, rhs[...] - jnp.where(down < k, col, 0.0) * x
            )
            return carry

        lax.fori_loop(0, R, backward, 0)
        out_ref[...] = rhs[...].T[0:ROWS]


def body(tensor, factor_b, factor_c):
    vmem = pl.BlockSpec(memory_space=pltpu.VMEM)
    hbm = pl.BlockSpec(memory_space=pltpu.HBM)
    dma, signal = pltpu.SemaphoreType.DMA, pltpu.SemaphoreType.REGULAR
    c_rows = jnp.pad(factor_c, ((0, 16 - KB), (0, JB - RC)))
    both = jnp.concatenate([factor_b.T, c_rows], axis=0)
    pack = pl.pallas_call(
        fused,
        out_shape=jax.ShapeDtypeStruct((G_AT + R, R), F32),
        in_specs=[hbm, pl.BlockSpec(memory_space=pl.ANY)],
        out_specs=vmem,
        scratch_shapes=[
            pltpu.VMEM((KB, IB, JB), BF16),
            pltpu.VMEM((NIA, RC + 16, JB), BF16),
            pltpu.VMEM((JB, R), BF16),
            pltpu.VMEM((NKA, 16, R), F32),
            pltpu.VMEM((R, R), F32),
            pltpu.VMEM((NJA, GROWS, R), F32),
            pltpu.VMEM((R, R), F32),
            pltpu.VMEM((NZ, BLOCK, R), F32),
            pltpu.VMEM((NZ, BLOCK, R), F32),
            pltpu.VMEM((NZ, NKA, ROWS, R), F32),
            pltpu.VMEM((NZ, NKA - 1, ROWS, R), F32),
            pltpu.VMEM((NZ, ROWS, R), F32),
            pltpu.VMEM((NZ, ROWS, R), F32),
            dma((NJA,)),
            dma, dma, dma, dma, dma, dma, dma, dma, dma,
            dma((NZ,)),
            dma((NZ,)),
            dma,
            dma((NZ,)),
            dma, dma,
            signal, signal, signal,
        ],
        compiler_params=pltpu.CompilerParams(
            collective_id=0, has_side_effects=True, vmem_limit_bytes=52 * 1024 * 1024
        ),
    )(tensor, both)
    return pl.pallas_call(
        finish,
        out_shape=jax.ShapeDtypeStruct((ROWS, R), F32),
        in_specs=[hbm],
        out_specs=vmem,
        scratch_shapes=[
            pltpu.VMEM((M_AT, R), F32),
            pltpu.VMEM((R, R), F32),
            pltpu.VMEM((R, R), F32),
            pltpu.VMEM((R, R), F32),
            dma((2,)),
        ],
        compiler_params=pltpu.CompilerParams(vmem_limit_bytes=8 * 1024 * 1024),
    )(pack)


def solution(mesh):
    return jax.shard_map(
        body,
        mesh=mesh,
        in_specs=(P("ka", "ia", "ja"), P("ja", "ia"), P("ka", "ia")),
        out_specs=P(("ia", "ja", "ka"), None),
        check_vma=False,
    )
```

```python
import jax
import jax.numpy as jnp
from jax import lax
from jax.experimental import pallas as pl
from jax.experimental.pallas import tpu as pltpu
from jax.sharding import PartitionSpec as P

LAMBDA_REG = 0.5
MESH = pl.DeviceIdType.MESH
F32 = jnp.float32
BF16 = jnp.bfloat16
EXACT = lax.Precision.HIGHEST

R = 128
NIA, NJA, NKA = 4, 16, 4
NZ = NJA // 2
RC = R // NIA
KB, IB, JB = 12, 1536, 256
ROWS = IB // (NJA * NKA)
BLOCK = ROWS * NKA
PAIR = 2
PLANE = NIA * PAIR
GROWS = R // PLANE
TERMS = 7
R_AT, M_AT, G_AT = ROWS, ROWS + 8, 2 * ROWS + 8
SURE = 2e-4


def nt(a, b):
    return lax.dot_general(a, b, (((1,), (1,)), ((), ())), preferred_element_type=F32)


def tn(a, b):
    return lax.dot_general(a, b, (((0,), (0,)), ((), ())), preferred_element_type=F32)


def exact(a, b):
    return jnp.dot(a, b, preferred_element_type=F32, precision=EXACT)


def eye():
    i = lax.broadcasted_iota(jnp.int32, (R, R), 0)
    j = lax.broadcasted_iota(jnp.int32, (R, R), 1)
    return (i == j).astype(F32)


def split(a):
    high = a.astype(BF16)
    return high, (a - high.astype(F32)).astype(BF16)


def mul3(a, b):
    both = jnp.concatenate(a, axis=1)
    twice = jnp.concatenate([b[0], b[0]], axis=0)
    return jnp.dot(both, twice, preferred_element_type=F32) + jnp.dot(
        a[0], b[1], preferred_element_type=F32
    )


def fused(
    t_hbm, bc, pack,
    t_v, gat, bfull, call, gpart, growin, gram,
    psend, precv, own, xin, zown, zin,
    t_sem, in_sem, a_send, a_recv, c_send, c_recv, g_send, g_recv, h_send, h_recv,
    p_send, p_recv, x_send, x_recv, z_send, z_recv, met_z, met_far, met_plane,
):
    ia, ja, ka = lax.axis_index("ia"), lax.axis_index("ja"), lax.axis_index("ka")
    z, core = ja // 2, lax.rem(ja, 2)
    other = 1 - core
    plane = ia * PAIR + lax.rem(ka, PAIR)
    left = []

    def at_y(o):
        return (lax.rem(ia + NIA + o, NIA), ja, ka)

    def at_x(o):
        return (ia, ja, lax.rem(ka + NKA + o, NKA))

    def at_z(o, c=core):
        return (ia, 2 * lax.rem(z + NZ + o, NZ) + c, ka)

    def tell(sem, device):
        pl.semaphore_signal(sem, inc=1, device_id=device, device_id_type=MESH)

    def others(me, n):
        return [t + (t >= me).astype(jnp.int32) for t in range(n - 1)]

    keep = pltpu.make_async_copy(bc, gat.at[ia], in_sem)
    keep.start()

    barrier = pltpu.get_barrier_semaphore()
    near = [at_y(o) for o in range(1, NIA)] + [at_z(0, other)]
    near += [at_z(o, c) for o in (1, -1) for c in (core, other)]
    near += [at_x(o) for o in range(1, NKA)]
    for device in near:
        tell(barrier, device)


    def slab_copy(i, c):
        rows = pl.ds(pl.multiple_of((2 * i + c) * BLOCK, BLOCK), BLOCK)
        return pltpu.make_async_copy(
            t_hbm.at[:, rows], t_v.at[:, rows], t_sem.at[jnp.where(c == other, i, NZ + i)]
        )

    loads = [pltpu.make_async_copy(t_hbm.at[k], t_v.at[k], t_sem.at[k]) for k in range(KB)]
    for load in loads:
        load.start(priority=1)

    pl.semaphore_wait(barrier, len(near))
    for y in reversed(others(ia, NIA)):
        pltpu.make_async_remote_copy(
            bc, gat.at[ia], a_send, a_recv, device_id=(y, ja, ka), device_id_type=MESH
        ).start()
    for o in (1, -1):
        tell(met_z, at_z(o))
    tell(met_plane, (ia, ja, ka + 1 - 2 * lax.rem(ka, PAIR)))
    pl.semaphore_wait(met_z, 2)
    for o in (2, -2):
        tell(met_far, at_z(o))
    keep.wait()
    three = gat.at[0 : NIA - 1]
    pltpu.make_async_copy(three, three, a_recv).wait()
    left.append(pltpu.make_async_copy(three, three, a_send).wait)

    bt = gat[:, 0:RC, :].reshape(R, JB)
    gpart[...] = nt(bt, bt)

    mine = pl.multiple_of(plane * GROWS, GROWS)
    pl.semaphore_wait(met_far, 2)

    growin[ja] = gpart[pl.ds(mine, GROWS), :]
    for to in others(ja, NJA):
        pltpu.make_async_remote_copy(
            growin.at[ja], growin.at[ja], g_send, g_recv,
            device_id=(ia, to, ka), device_id_type=MESH,
        ).start()
    crows = jnp.concatenate([gat[i, RC:, 0:RC].astype(F32) for i in range(NIA)], axis=1)
    call[ka] = crows
    for o in range(1, NKA):
        pltpu.make_async_remote_copy(
            call.at[ka], call.at[ka], c_send, c_recv, device_id=at_x(o), device_id_type=MESH
        ).start()
    left.append(pltpu.make_async_copy(growin.at[1:], growin.at[1:], g_send).wait)
    left.append(pltpu.make_async_copy(call.at[0:3], call.at[0:3], c_send).wait)

    bfull[...] = bt.astype(F32).T.astype(BF16)
    b_all = bfull[...]
    scales = [crows[k : k + 1] for k in range(KB)]

    def contract(rows):
        t = t_v[:, pl.ds(rows, BLOCK), :].reshape(KB * BLOCK, JB)
        products = jnp.dot(t, b_all, preferred_element_type=F32)
        total = products[0:BLOCK] * scales[0]
        for k in range(1, KB):
            total = total + products[k * BLOCK : (k + 1) * BLOCK] * scales[k]
        return total

    def pair_copy(i):
        return pltpu.make_async_remote_copy(
            psend.at[i], precv.at[i], p_send.at[i], p_recv.at[i],
            device_id=(ia, 2 * z + other, ka), device_id_type=MESH,
        )

    def sibling_block(i, carry):
        psend[i] = contract(pl.multiple_of((2 * i + other) * BLOCK, BLOCK))
        pair_copy(i).start()
        return carry

    for load in loads:
        load.wait()
    lax.fori_loop(0, NZ, sibling_block, 0)
    left.append(lambda: [pair_copy(i).wait_send() for i in range(NZ)])

    def own_block(i, carry):
        total = contract(pl.multiple_of((2 * i + core) * BLOCK, BLOCK))
        pair_copy(i).wait_recv()
        own[i] = (total + precv[i]).reshape(NKA, ROWS, R)
        for t, to in enumerate(others(ka, NKA)):
            pltpu.make_async_remote_copy(
                own.at[i, to], xin.at[i, ka - (ka > to).astype(jnp.int32)],
                x_send, x_recv.at[i], device_id=(ia, ja, to), device_id_type=MESH,
            ).start()
        return carry

    lax.fori_loop(0, NZ, own_block, 0)
    left.append(pltpu.make_async_copy(xin, xin, x_send).wait)

    def forward(i, carry):
        pltpu.make_async_copy(xin.at[i], xin.at[i], x_recv.at[i]).wait()
        zown[i] = own[i, ka] + (xin[i, 0] + xin[i, 1] + xin[i, 2])

        @pl.when(i != z)
        def _():
            pltpu.make_async_remote_copy(
                zown.at[i], zin.at[z], z_send, z_recv,
                device_id=(ia, 2 * i + core, ka), device_id_type=MESH,
            ).start()

        return carry

    pltpu.make_async_copy(growin.at[1:], growin.at[1:], g_recv).wait()
    rows = growin[0]
    for o in range(1, NJA):
        rows = rows + growin[o]
    gram[pl.ds(mine, GROWS), :] = rows
    pl.semaphore_wait(met_plane, 1)
    for p in others(plane, PLANE):
        pltpu.make_async_remote_copy(
            gram.at[pl.ds(mine, GROWS)], gram.at[pl.ds(mine, GROWS)], h_send, h_recv,
            device_id=(p // PAIR, ja, ka // PAIR * PAIR + lax.rem(p, PAIR)), device_id_type=MESH,
        ).start()
    left.append(pltpu.make_async_copy(gram.at[0 : R - GROWS], gram.at[0 : R - GROWS], h_send).wait)
    lax.fori_loop(0, NZ, forward, 0)
    left.append(pltpu.make_async_copy(zin.at[1:], zin.at[1:], z_send).wait)

    pltpu.make_async_copy(gram.at[0 : R - GROWS], gram.at[0 : R - GROWS], h_recv).wait()
    pltpu.make_async_copy(call.at[0:3], call.at[0:3], c_recv).wait()
    every = call[...].reshape(NKA * 16, R).astype(BF16)
    one = eye()
    g = gram[...] * tn(every, every) + LAMBDA_REG * one
    pack[G_AT:, :] = g
    size = jnp.abs(g)
    across = jnp.sum(size, axis=0, keepdims=True)
    down = jnp.sum(size, axis=1, keepdims=True)
    bound = jnp.max(jnp.sum(size * across, axis=1, keepdims=True) / down, axis=0, keepdims=True)
    alpha = 2.0 / (bound + LAMBDA_REG)
    e = one - alpha * g
    p = one + e
    for _ in range(TERMS - 1):
        parts = split(e)
        e = mul3(parts, parts)
        p = p + mul3(split(p), split(e))
    inv = alpha * p
    rest = one - exact(g, inv)
    pack[R_AT : R_AT + 8, :] = jnp.broadcast_to(
        jnp.max(jnp.sum(jnp.abs(rest), axis=0, keepdims=True), axis=1, keepdims=True), (8, R)
    )
    inv = inv + mul3(split(inv), split(rest))

    zin[z] = zown[z]
    pltpu.make_async_copy(zin.at[1:], zin.at[1:], z_recv).wait()
    rows = zin[0]
    for o in range(1, NZ):
        rows = rows + zin[o]
    pack[M_AT : M_AT + ROWS, :] = rows
    pack[0:ROWS, :] = exact(rows, inv)
    for wait in left:
        wait()


def finish(pack, out_ref, head, mat, rhs, upper, sem):
    load = pltpu.make_async_copy(pack.at[0:M_AT], head, sem.at[0])
    load.start()
    load.wait()
    sure = jnp.max(head[R_AT:M_AT, :]) < SURE

    @pl.when(sure)
    def _():
        out_ref[...] = head[0:ROWS, :]

    @pl.when(jnp.logical_not(sure))
    def _():
        rhs[...] = jnp.zeros((R, R), F32)
        load_g = pltpu.make_async_copy(pack.at[G_AT:], mat, sem.at[0])
        load_m = pltpu.make_async_copy(pack.at[M_AT:G_AT], rhs.at[0:ROWS], sem.at[1])
        load_g.start()
        load_m.start()
        load_g.wait()
        load_m.wait()
        rhs[...] = rhs[...].T
        down = lax.broadcasted_iota(jnp.int32, (R, 1), 0)
        across = lax.broadcasted_iota(jnp.int32, (1, R), 1)

        def column(a, k):
            return jnp.sum(jnp.where(across == k, a, 0.0), axis=1, keepdims=True)

        def forward(k, carry):
            a = mat[...]
            row = mat[pl.ds(k, 1), :]
            root = jnp.sqrt(jnp.sum(jnp.where(across == k, row, 0.0), axis=1, keepdims=True))
            lrow = jnp.where(across >= k, row / root, 0.0)
            lcol = jnp.where(down > k, column(a, k) / root, 0.0)
            upper[pl.ds(k, 1), :] = lrow
            mat[...] = a - lcol * lrow
            b = rhs[pl.ds(k, 1), :] / root
            rhs[...] = jnp.where(down == k, b, rhs[...] - lcol * b)
            return carry

        lax.fori_loop(0, R, forward, 0)

        def backward(step, carry):
            k = R - 1 - step
            col = column(upper[...], k)
            root = jnp.sum(jnp.where(down == k, col, 0.0), axis=0, keepdims=True)
            x = rhs[pl.ds(k, 1), :] / root
            rhs[...] = jnp.where(
                down == k, x, rhs[...] - jnp.where(down < k, col, 0.0) * x
            )
            return carry

        lax.fori_loop(0, R, backward, 0)
        out_ref[...] = rhs[...].T[0:ROWS]


def body(tensor, factor_b, factor_c):
    vmem = pl.BlockSpec(memory_space=pltpu.VMEM)
    hbm = pl.BlockSpec(memory_space=pltpu.HBM)
    dma, signal = pltpu.SemaphoreType.DMA, pltpu.SemaphoreType.REGULAR
    c_rows = jnp.pad(factor_c, ((0, 16 - KB), (0, JB - RC)))
    both = jnp.concatenate([factor_b.T, c_rows], axis=0)
    pack = pl.pallas_call(
        fused,
        out_shape=jax.ShapeDtypeStruct((G_AT + R, R), F32),
        in_specs=[hbm, pl.BlockSpec(memory_space=pl.ANY)],
        out_specs=vmem,
        scratch_shapes=[
            pltpu.VMEM((KB, IB, JB), BF16),
            pltpu.VMEM((NIA, RC + 16, JB), BF16),
            pltpu.VMEM((JB, R), BF16),
            pltpu.VMEM((NKA, 16, R), F32),
            pltpu.VMEM((R, R), F32),
            pltpu.VMEM((NJA, GROWS, R), F32),
            pltpu.VMEM((R, R), F32),
            pltpu.VMEM((NZ, BLOCK, R), F32),
            pltpu.VMEM((NZ, BLOCK, R), F32),
            pltpu.VMEM((NZ, NKA, ROWS, R), F32),
            pltpu.VMEM((NZ, NKA - 1, ROWS, R), F32),
            pltpu.VMEM((NZ, ROWS, R), F32),
            pltpu.VMEM((NZ, ROWS, R), F32),
            dma((NJA,)),
            dma, dma, dma, dma, dma, dma, dma, dma, dma,
            dma((NZ,)),
            dma((NZ,)),
            dma,
            dma((NZ,)),
            dma, dma,
            signal, signal, signal,
        ],
        compiler_params=pltpu.CompilerParams(
            collective_id=0, has_side_effects=True, vmem_limit_bytes=52 * 1024 * 1024
        ),
    )(tensor, both)
    return pl.pallas_call(
        finish,
        out_shape=jax.ShapeDtypeStruct((ROWS, R), F32),
        in_specs=[hbm],
        out_specs=vmem,
        scratch_shapes=[
            pltpu.VMEM((M_AT, R), F32),
            pltpu.VMEM((R, R), F32),
            pltpu.VMEM((R, R), F32),
            pltpu.VMEM((R, R), F32),
            dma((2,)),
        ],
        compiler_params=pltpu.CompilerParams(vmem_limit_bytes=8 * 1024 * 1024),
    )(pack)


def solution(mesh):
    return jax.shard_map(
        body,
        mesh=mesh,
        in_specs=(P("ka", "ia", "ja"), P("ja", "ia"), P("ka", "ia")),
        out_specs=P(("ia", "ja", "ka"), None),
        check_vma=False,
    )
```

```python
import jax
import jax.numpy as jnp
from jax import lax
from jax.experimental import pallas as pl
from jax.experimental.pallas import tpu as pltpu
from jax.sharding import PartitionSpec as P

LAMBDA_REG = 0.5
MESH = pl.DeviceIdType.MESH
F32 = jnp.float32
BF16 = jnp.bfloat16
EXACT = lax.Precision.HIGHEST

R = 128
NIA, NJA, NKA = 4, 16, 4
NZ = NJA // 2
RC = R // NIA
KB, IB, JB = 12, 1536, 256
ROWS = IB // (NJA * NKA)
BLOCK = ROWS * NKA
PAIR = 2
PLANE = NIA * PAIR
GROWS = R // PLANE
TERMS = 7
R_AT, M_AT, G_AT = ROWS, ROWS + 8, 2 * ROWS + 8
SURE = 2e-4


def nt(a, b):
    return lax.dot_general(a, b, (((1,), (1,)), ((), ())), preferred_element_type=F32)


def tn(a, b):
    return lax.dot_general(a, b, (((0,), (0,)), ((), ())), preferred_element_type=F32)


def exact(a, b):
    return jnp.dot(a, b, preferred_element_type=F32, precision=EXACT)


def eye():
    i = lax.broadcasted_iota(jnp.int32, (R, R), 0)
    j = lax.broadcasted_iota(jnp.int32, (R, R), 1)
    return (i == j).astype(F32)


def split(a):
    high = a.astype(BF16)
    return high, (a - high.astype(F32)).astype(BF16)


def mul3(a, b):
    both = jnp.concatenate(a, axis=1)
    twice = jnp.concatenate([b[0], b[0]], axis=0)
    return jnp.dot(both, twice, preferred_element_type=F32) + jnp.dot(
        a[0], b[1], preferred_element_type=F32
    )


def fused(
    t_hbm, bc, pack,
    t_v, gat, bfull, call, growin, gram,
    psend, precv, own, xin, zown, zin,
    t_sem, in_sem, a_send, a_recv, c_send, c_recv, g_send, g_recv, h_send, h_recv,
    p_send, p_recv, x_send, x_recv, z_send, z_recv, met_z, met_far, met_plane,
):
    ia, ja, ka = lax.axis_index("ia"), lax.axis_index("ja"), lax.axis_index("ka")
    z, core = ja // 2, lax.rem(ja, 2)
    other = 1 - core
    plane = ia * PAIR + lax.rem(ka, PAIR)
    left = []

    def at_y(o):
        return (lax.rem(ia + NIA + o, NIA), ja, ka)

    def at_x(o):
        return (ia, ja, lax.rem(ka + NKA + o, NKA))

    def at_z(o, c=core):
        return (ia, 2 * lax.rem(z + NZ + o, NZ) + c, ka)

    def tell(sem, device):
        pl.semaphore_signal(sem, inc=1, device_id=device, device_id_type=MESH)

    def others(me, n):
        return [t + (t >= me).astype(jnp.int32) for t in range(n - 1)]

    keep = pltpu.make_async_copy(bc, gat.at[ia], in_sem)
    keep.start()

    barrier = pltpu.get_barrier_semaphore()
    near = [at_y(o) for o in range(1, NIA)] + [at_z(0, other)]
    near += [at_z(o, c) for o in (1, -1) for c in (core, other)]
    near += [at_x(o) for o in range(1, NKA)]
    for device in near:
        tell(barrier, device)


    def slab_copy(i, c):
        rows = pl.ds(pl.multiple_of((2 * i + c) * BLOCK, BLOCK), BLOCK)
        return pltpu.make_async_copy(
            t_hbm.at[:, rows], t_v.at[:, rows], t_sem.at[jnp.where(c == other, i, NZ + i)]
        )

    loads = [pltpu.make_async_copy(t_hbm.at[k], t_v.at[k], t_sem.at[k]) for k in range(KB)]
    for load in loads:
        load.start(priority=1)

    pl.semaphore_wait(barrier, len(near))
    for y in reversed(others(ia, NIA)):
        pltpu.make_async_remote_copy(
            bc, gat.at[ia], a_send, a_recv, device_id=(y, ja, ka), device_id_type=MESH
        ).start()
    for o in (1, -1):
        tell(met_z, at_z(o))
    tell(met_plane, (ia, ja, ka + 1 - 2 * lax.rem(ka, PAIR)))
    pl.semaphore_wait(met_z, 2)
    for o in (2, -2):
        tell(met_far, at_z(o))
    keep.wait()
    three = gat.at[0 : NIA - 1]
    pltpu.make_async_copy(three, three, a_recv).wait()
    left.append(pltpu.make_async_copy(three, three, a_send).wait)

    bt = gat[:, 0:RC, :].reshape(R, JB)

    mine = pl.multiple_of(plane * GROWS, GROWS)
    pl.semaphore_wait(met_far, 2)

    growin[ja] = nt(gat[ia, pl.ds(pl.multiple_of(lax.rem(ka, PAIR) * GROWS, GROWS), GROWS), :], bt)
    for to in others(ja, NJA):
        pltpu.make_async_remote_copy(
            growin.at[ja], growin.at[ja], g_send, g_recv,
            device_id=(ia, to, ka), device_id_type=MESH,
        ).start()
    crows = jnp.concatenate([gat[i, RC:, 0:RC].astype(F32) for i in range(NIA)], axis=1)
    call[ka] = crows
    for o in range(1, NKA):
        pltpu.make_async_remote_copy(
            call.at[ka], call.at[ka], c_send, c_recv, device_id=at_x(o), device_id_type=MESH
        ).start()
    left.append(pltpu.make_async_copy(growin.at[1:], growin.at[1:], g_send).wait)
    left.append(pltpu.make_async_copy(call.at[0:3], call.at[0:3], c_send).wait)

    bfull[...] = bt.astype(F32).T.astype(BF16)
    b_all = bfull[...]
    scales = [crows[k : k + 1] for k in range(KB)]

    def contract(rows):
        t = t_v[:, pl.ds(rows, BLOCK), :].reshape(KB * BLOCK, JB)
        products = jnp.dot(t, b_all, preferred_element_type=F32)
        total = products[0:BLOCK] * scales[0]
        for k in range(1, KB):
            total = total + products[k * BLOCK : (k + 1) * BLOCK] * scales[k]
        return total

    def pair_copy(i):
        return pltpu.make_async_remote_copy(
            psend.at[i], precv.at[i], p_send.at[i], p_recv.at[i],
            device_id=(ia, 2 * z + other, ka), device_id_type=MESH,
        )

    def sibling_block(i, carry):
        psend[i] = contract(pl.multiple_of((2 * i + other) * BLOCK, BLOCK))
        pair_copy(i).start()
        return carry

    for load in loads:
        load.wait()
    lax.fori_loop(0, NZ, sibling_block, 0)
    left.append(lambda: [pair_copy(i).wait_send() for i in range(NZ)])

    def own_block(i, carry):
        total = contract(pl.multiple_of((2 * i + core) * BLOCK, BLOCK))
        pair_copy(i).wait_recv()
        own[i] = (total + precv[i]).reshape(NKA, ROWS, R)
        for t, to in enumerate(others(ka, NKA)):
            pltpu.make_async_remote_copy(
                own.at[i, to], xin.at[i, ka - (ka > to).astype(jnp.int32)],
                x_send, x_recv.at[i], device_id=(ia, ja, to), device_id_type=MESH,
            ).start()
        return carry

    lax.fori_loop(0, NZ, own_block, 0)
    left.append(pltpu.make_async_copy(xin, xin, x_send).wait)

    def forward(i, carry):
        pltpu.make_async_copy(xin.at[i], xin.at[i], x_recv.at[i]).wait()
        zown[i] = own[i, ka] + (xin[i, 0] + xin[i, 1] + xin[i, 2])

        @pl.when(i != z)
        def _():
            pltpu.make_async_remote_copy(
                zown.at[i], zin.at[z], z_send, z_recv,
                device_id=(ia, 2 * i + core, ka), device_id_type=MESH,
            ).start()

        return carry

    pltpu.make_async_copy(growin.at[1:], growin.at[1:], g_recv).wait()
    rows = growin[0]
    for o in range(1, NJA):
        rows = rows + growin[o]
    gram[pl.ds(mine, GROWS), :] = rows
    pl.semaphore_wait(met_plane, 1)
    for p in others(plane, PLANE):
        pltpu.make_async_remote_copy(
            gram.at[pl.ds(mine, GROWS)], gram.at[pl.ds(mine, GROWS)], h_send, h_recv,
            device_id=(p // PAIR, ja, ka // PAIR * PAIR + lax.rem(p, PAIR)), device_id_type=MESH,
        ).start()
    left.append(pltpu.make_async_copy(gram.at[0 : R - GROWS], gram.at[0 : R - GROWS], h_send).wait)
    lax.fori_loop(0, NZ, forward, 0)
    left.append(pltpu.make_async_copy(zin.at[1:], zin.at[1:], z_send).wait)

    pltpu.make_async_copy(gram.at[0 : R - GROWS], gram.at[0 : R - GROWS], h_recv).wait()
    pltpu.make_async_copy(call.at[0:3], call.at[0:3], c_recv).wait()
    every = call[...].reshape(NKA * 16, R).astype(BF16)
    one = eye()
    g = gram[...] * tn(every, every) + LAMBDA_REG * one
    pack[G_AT:, :] = g
    size = jnp.abs(g)
    across = jnp.sum(size, axis=0, keepdims=True)
    down = jnp.sum(size, axis=1, keepdims=True)
    bound = jnp.max(jnp.sum(size * across, axis=1, keepdims=True) / down, axis=0, keepdims=True)
    alpha = 2.0 / (bound + LAMBDA_REG)
    e = one - alpha * g
    p = one + e
    for _ in range(TERMS - 1):
        parts = split(e)
        e = mul3(parts, parts)
        p = p + mul3(split(p), split(e))
    inv = alpha * p
    rest = one - exact(g, inv)
    pack[R_AT : R_AT + 8, :] = jnp.broadcast_to(
        jnp.max(jnp.sum(jnp.abs(rest), axis=0, keepdims=True), axis=1, keepdims=True), (8, R)
    )
    inv = inv + mul3(split(inv), split(rest))

    zin[z] = zown[z]
    pltpu.make_async_copy(zin.at[1:], zin.at[1:], z_recv).wait()
    rows = zin[0]
    for o in range(1, NZ):
        rows = rows + zin[o]
    pack[M_AT : M_AT + ROWS, :] = rows
    pack[0:ROWS, :] = exact(rows, inv)
    for wait in left:
        wait()


def finish(pack, out_ref, head, mat, rhs, upper, sem):
    load = pltpu.make_async_copy(pack.at[0:M_AT], head, sem.at[0])
    load.start()
    load.wait()
    sure = jnp.max(head[R_AT:M_AT, :]) < SURE

    @pl.when(sure)
    def _():
        out_ref[...] = head[0:ROWS, :]

    @pl.when(jnp.logical_not(sure))
    def _():
        rhs[...] = jnp.zeros((R, R), F32)
        load_g = pltpu.make_async_copy(pack.at[G_AT:], mat, sem.at[0])
        load_m = pltpu.make_async_copy(pack.at[M_AT:G_AT], rhs.at[0:ROWS], sem.at[1])
        load_g.start()
        load_m.start()
        load_g.wait()
        load_m.wait()
        rhs[...] = rhs[...].T
        down = lax.broadcasted_iota(jnp.int32, (R, 1), 0)
        across = lax.broadcasted_iota(jnp.int32, (1, R), 1)

        def column(a, k):
            return jnp.sum(jnp.where(across == k, a, 0.0), axis=1, keepdims=True)

        def forward(k, carry):
            a = mat[...]
            row = mat[pl.ds(k, 1), :]
            root = jnp.sqrt(jnp.sum(jnp.where(across == k, row, 0.0), axis=1, keepdims=True))
            lrow = jnp.where(across >= k, row / root, 0.0)
            lcol = jnp.where(down > k, column(a, k) / root, 0.0)
            upper[pl.ds(k, 1), :] = lrow
            mat[...] = a - lcol * lrow
            b = rhs[pl.ds(k, 1), :] / root
            rhs[...] = jnp.where(down == k, b, rhs[...] - lcol * b)
            return carry

        lax.fori_loop(0, R, forward, 0)

        def backward(step, carry):
            k = R - 1 - step
            col = column(upper[...], k)
            root = jnp.sum(jnp.where(down == k, col, 0.0), axis=0, keepdims=True)
            x = rhs[pl.ds(k, 1), :] / root
            rhs[...] = jnp.where(
                down == k, x, rhs[...] - jnp.where(down < k, col, 0.0) * x
            )
            return carry

        lax.fori_loop(0, R, backward, 0)
        out_ref[...] = rhs[...].T[0:ROWS]


def body(tensor, factor_b, factor_c):
    vmem = pl.BlockSpec(memory_space=pltpu.VMEM)
    hbm = pl.BlockSpec(memory_space=pltpu.HBM)
    dma, signal = pltpu.SemaphoreType.DMA, pltpu.SemaphoreType.REGULAR
    c_rows = jnp.pad(factor_c, ((0, 16 - KB), (0, JB - RC)))
    both = jnp.concatenate([factor_b.T, c_rows], axis=0)
    pack = pl.pallas_call(
        fused,
        out_shape=jax.ShapeDtypeStruct((G_AT + R, R), F32),
        in_specs=[hbm, pl.BlockSpec(memory_space=pl.ANY)],
        out_specs=vmem,
        scratch_shapes=[
            pltpu.VMEM((KB, IB, JB), BF16),
            pltpu.VMEM((NIA, RC + 16, JB), BF16),
            pltpu.VMEM((JB, R), BF16),
            pltpu.VMEM((NKA, 16, R), F32),
            pltpu.VMEM((NJA, GROWS, R), F32),
            pltpu.VMEM((R, R), F32),
            pltpu.VMEM((NZ, BLOCK, R), F32),
            pltpu.VMEM((NZ, BLOCK, R), F32),
            pltpu.VMEM((NZ, NKA, ROWS, R), F32),
            pltpu.VMEM((NZ, NKA - 1, ROWS, R), F32),
            pltpu.VMEM((NZ, ROWS, R), F32),
            pltpu.VMEM((NZ, ROWS, R), F32),
            dma((NJA,)),
            dma, dma, dma, dma, dma, dma, dma, dma, dma,
            dma((NZ,)),
            dma((NZ,)),
            dma,
            dma((NZ,)),
            dma, dma,
            signal, signal, signal,
        ],
        compiler_params=pltpu.CompilerParams(
            collective_id=0, has_side_effects=True, vmem_limit_bytes=52 * 1024 * 1024
        ),
    )(tensor, both)
    return pl.pallas_call(
        finish,
        out_shape=jax.ShapeDtypeStruct((ROWS, R), F32),
        in_specs=[hbm],
        out_specs=vmem,
        scratch_shapes=[
            pltpu.VMEM((M_AT, R), F32),
            pltpu.VMEM((R, R), F32),
            pltpu.VMEM((R, R), F32),
            pltpu.VMEM((R, R), F32),
            dma((2,)),
        ],
        compiler_params=pltpu.CompilerParams(vmem_limit_bytes=8 * 1024 * 1024),
    )(pack)


def solution(mesh):
    return jax.shard_map(
        body,
        mesh=mesh,
        in_specs=(P("ka", "ia", "ja"), P("ja", "ia"), P("ka", "ia")),
        out_specs=P(("ia", "ja", "ka"), None),
        check_vma=False,
    )
```
